256 devices in a mesh: ep: 16 (over z, y_hi), dp: 16 (over y_lo, x, core).
Axes of the slice: x: 4, y: 4 (y_hi: 2, y_lo: 2; y = y_hi * 2 + y_lo), z: 8, core: 2. Of those that a mesh axis runs over, the one named last changes fastest.
Arguments:
- route_experts: int32 [65536, 6], P(('ep', 'dp')), may hold values from 0 to 159, as said below
- route_slots: int32 [65536, 6], P(('ep', 'dp')), may hold values from 0 to 255, as said below
- shared_grad: bfloat16 [65536, 2560], P(('ep', 'dp')), may hold values from -6 to 6
- counts: int32 [16, 256], P('ep', 'dp'), may hold values from 0 to 24, as said below
- slot_inputs: bfloat16 [16, 6144, 2560], P('ep', 'dp'), may hold values from -6 to 6
- gate_pre: bfloat16 [16, 6144, 768], P('ep', 'dp'), may hold values from -6 to 6
- up_pre: bfloat16 [16, 6144, 768], P('ep', 'dp'), may hold values from -6 to 6
- hidden_grad: bfloat16 [16, 6144, 768], P('ep', 'dp'), may hold values from -6 to 6
- slot_prob: float32 [16, 6144], P('ep', 'dp'), may hold values from 0.1 to 1
- gate_master: float32 [16, 2560, 768], P('ep', 'dp'), may hold values from -0.125 to 0.125
- gate_first: bfloat16 [16, 2560, 768], P('ep', 'dp'), may hold values from -18 to 18
- gate_second: bfloat16 [16, 2560, 768], P('ep', 'dp'), may hold values from 0.5 to 20
- up_weight: bfloat16 [16, 2560, 768], P('ep', 'dp'), may hold values from -0.125 to 0.125
Outputs:
- grad_input: bfloat16 [65536, 2560], P(('ep', 'dp'))
- score_grad: bfloat16 [65536, 6], P(('ep', 'dp'))
- new_master: float32 [16, 2560, 768], P('ep', 'dp')
- new_first: bfloat16 [16, 2560, 768], P('ep', 'dp')
- new_second: bfloat16 [16, 2560, 768], P('ep', 'dp')
- new_weights: bfloat16 [16, 2560, 768], P('ep')
The draws below stay inside these ranges and needn't reach their ends.
Inputs may be any that keep to these rules, and one draw needn't show every extreme that they name: `route_experts`: each token names 6 different experts of the 160; every expert is named by some token; expert x below 16 is held by ep index x. `route_slots`: the number of earlier tokens of the same device that name the same expert; some device has an expert named by all its 256 tokens. `counts`: entry [x, d * 16 + s] is the number of choices of expert x by tokens of the device at ep index s and dp index d with rank below 24, that is min(24, all such choices). For every dp index some expert holds exactly 24 rows from every device. Rows of a block past its count belong to no token.
All inputs are finite; a program needn't handle non-finite values.
Results may differ from the reference program's by a relative error of at most 0.0049.
Values may be sent and summed in bfloat16 or wider, within the bound.
A program may use at most 128 MiB of HBM per device.

```python
import math
import jax
import jax.numpy as jnp
from jax import lax

D = 2560
H = 768
ALL_EXPERTS = 160
TOP = 6
TOK_DEV = 256
CAP = 24
EXPERTS = 16
TOKENS = 65536
N_EP = 16
N_DP = 16


def routing_tables(key):
    blocks = N_EP * N_DP
    score_key, hot_key, order_key = jax.random.split(key, 3)
    raw_scores = jax.random.randint(score_key, (blocks, TOK_DEV, ALL_EXPERTS), 0, 2 ** 20)
    expert_index_list = lax.broadcasted_iota(jnp.int32, (blocks, TOK_DEV, ALL_EXPERTS), 2)
    router_scores = raw_scores * 256 + expert_index_list
    hot_expert = jax.random.randint(hot_key, (N_DP,), 0, EXPERTS)
    block_ids = jnp.arange(blocks, dtype=jnp.int32)
    group = block_ids % N_DP
    favored_block = hot_expert[group]
    orders = jax.vmap(lambda sub: jax.random.permutation(sub, TOK_DEV))(jax.random.split(order_key, blocks))
    raised_scores = (orders < CAP) | (block_ids[:, None] == 0)
    extra_logit = jnp.where(raised_scores[:, :, None] & (expert_index_list == favored_block[:, None, None]), 2 ** 29, 0)
    token_ids = lax.broadcasted_iota(jnp.int32, (blocks, TOK_DEV), 1)
    forced = (block_ids[:, None] * TOK_DEV + token_ids) % ALL_EXPERTS
    expert_coverage = jnp.where(expert_index_list == forced[:, :, None], 2 ** 28, 0)
    grand_sum = router_scores + extra_logit + expert_coverage
    top_scores, top_index = lax.top_k(grand_sum, TOP)
    chosen = (top_scores % 256).astype(jnp.int32)
    selected = (grand_sum >= top_scores[:, :, TOP - 1:TOP]).astype(jnp.int32)
    before = jnp.cumsum(selected, axis=1) - selected
    ranks = jnp.take_along_axis(before, chosen, axis=2)
    demand = jnp.sum(selected, axis=1)
    return (chosen, ranks, demand)


def draw_route_experts(key, part):
    chosen, ranks, demand = routing_tables(key)
    return chosen.reshape(TOKENS, TOP).astype(jnp.int32)


def draw_route_slots(key, part):
    chosen, ranks, demand = routing_tables(key)
    return ranks.reshape(TOKENS, TOP).astype(jnp.int32)


def draw_counts(key, part):
    chosen, ranks, demand = routing_tables(key)
    held = jnp.minimum(demand[:, :EXPERTS], CAP)
    held = held.reshape(N_EP, N_DP, EXPERTS).transpose(2, 1, 0)
    return held.reshape(EXPERTS, N_DP * N_EP).astype(jnp.int32)


def level_of(key, dims, shards, smallest, largest):
    factor_of = 1.0
    for axis_at, blocks in shards:
        steps = jax.random.uniform(jax.random.fold_in(jax.random.fold_in(key, 6), axis_at), (blocks,), jnp.float32, smallest / len(shards), largest / len(shards))
        factor_of = factor_of * jnp.repeat(jnp.exp(steps), dims[axis_at] // blocks).reshape((-1,) + (1,) * (len(dims) - 1 - axis_at))
    return factor_of


def gaussian(stream_key, extent, spread, reach, cuts=(), kind=jnp.bfloat16):
    array = jax.random.normal(stream_key, extent, jnp.float32) * spread
    if len(cuts) > 0:
        array = level_of(stream_key, extent, cuts, -0.22, 0.18) * array
    return jnp.clip(array, min=-reach, max=reach).astype(kind)


def setup_inputs(seed: int = 0) -> dict:
    splits = jax.random.split(jax.random.key(seed), 14)
    route_experts = draw_route_experts(jax.random.fold_in(splits[13], 71), 0)
    route_slots = draw_route_slots(jax.random.fold_in(splits[13], 71), 0)
    shared_grad = gaussian(splits[2], (TOKENS, D), 1.0, 6.0, ((0, 256),))
    counts = draw_counts(jax.random.fold_in(splits[13], 71), 0)
    slot_inputs = gaussian(splits[4], (EXPERTS, N_DP * N_EP * CAP, D), 1.0, 6.0, ((0, 16), (1, 16)))
    gate_pre = gaussian(splits[5], (EXPERTS, N_DP * N_EP * CAP, H), 1.0, 6.0, ((0, 16), (1, 16)))
    up_pre = gaussian(splits[6], (EXPERTS, N_DP * N_EP * CAP, H), 1.0, 6.0, ((0, 16), (1, 16)))
    hidden_grad = gaussian(splits[7], (EXPERTS, N_DP * N_EP * CAP, H), 1.0, 6.0, ((0, 16), (1, 16)))
    slot_prob = jnp.clip(jnp.exp(math.log(1.0) - 2.3025851 * jax.random.uniform(splits[8], (EXPERTS, N_DP * N_EP * CAP), jnp.float32) ** level_of(splits[8], (EXPERTS, N_DP * N_EP * CAP), ((0, 16), (1, 16)), -0.2, 0.2)), 0.1, 1.0)
    gate_master = gaussian(splits[9], (EXPERTS, D, H), D ** -0.5, 0.125, ((0, 16), (1, 16)), jnp.float32)
    gate_first = gaussian(splits[10], (EXPERTS, D, H), 3.0, 18.0, ((0, 16), (1, 16)))
    gate_second = jnp.clip(jnp.exp(math.log(20.0) - 3.6888795 * jax.random.uniform(splits[11], (EXPERTS, D, H), jnp.float32) ** level_of(splits[11], (EXPERTS, D, H), ((0, 16), (1, 16)), -0.2, 0.2)), 0.5, 20.0).astype(jnp.bfloat16)
    up_weight = gaussian(splits[12], (EXPERTS, D, H), D ** -0.5, 0.125, ((0, 16), (1, 16)))
    return {"route_experts": route_experts, "route_slots": route_slots, "shared_grad": shared_grad, "counts": counts, "slot_inputs": slot_inputs, "gate_pre": gate_pre, "up_pre": up_pre, "hidden_grad": hidden_grad, "slot_prob": slot_prob, "gate_master": gate_master, "gate_first": gate_first, "gate_second": gate_second, "up_weight": up_weight}


first_decay = 0.9
second_decay = 0.95
learn_rate = 0.001
weight_decay = 0.1
adam_eps = 1e-08
first_fix = 1.0 - 0.9 ** 10
second_fix = 1.0 - 0.95 ** 10

def slot_backward(gate_rows, up_rows, grad_rows, prob_rows):
    gate_value = gate_rows.astype(jnp.float32)
    up_value = up_rows.astype(jnp.float32)
    grad_value = grad_rows.astype(jnp.float32)
    gate_sig = jax.nn.sigmoid(gate_value)
    gate_act = gate_value * gate_sig
    slot_score = lax.optimization_barrier(jnp.sum(grad_value * gate_act * up_value, axis=-1)).astype(jnp.bfloat16)
    scaled = prob_rows[:, None] * grad_value
    d_up = (scaled * gate_act).astype(jnp.bfloat16)
    d_gate = (scaled * up_value * gate_sig * (1.0 + gate_value * (1.0 - gate_sig))).astype(jnp.bfloat16)
    return (d_gate, d_up, slot_score)

def reference(route_experts, route_slots, shared_grad, counts, slot_inputs, gate_pre, up_pre, hidden_grad, slot_prob, gate_master, gate_first, gate_second, up_weight):
    rows_all = N_DP * N_EP * CAP
    position = jnp.arange(rows_all, dtype=jnp.int32)

    def per_expert(packed):
        x_rows, gate_rows, up_rows, grad_rows, prob_rows, held, master, up_w = packed
        live_rows = position % CAP < jnp.repeat(held, CAP, total_repeat_length=rows_all)
        d_gate, d_up, slot_score = slot_backward(gate_rows, up_rows, grad_rows, prob_rows)
        d_gate = jnp.where(live_rows[:, None], d_gate, jnp.zeros_like(d_gate))
        d_up = jnp.where(live_rows[:, None], d_up, jnp.zeros_like(d_up))
        gate_w = master.astype(jnp.bfloat16)
        slot_grad = (jnp.dot(d_gate, gate_w.T, preferred_element_type=jnp.float32) + jnp.dot(d_up, up_w.T, preferred_element_type=jnp.float32)).astype(jnp.bfloat16)
        weight_grad = jnp.dot(x_rows.T, d_gate, preferred_element_type=jnp.float32)
        return (slot_grad, slot_score, weight_grad)
    slot_grad, slot_score, weight_grad = lax.map(per_expert, (slot_inputs, gate_pre, up_pre, hidden_grad, slot_prob, counts, gate_master, up_weight))
    moment_one = first_decay * gate_first.astype(jnp.float32) + (1.0 - first_decay) * weight_grad
    moment_two = second_decay * gate_second.astype(jnp.float32) + (1.0 - second_decay) * weight_grad * weight_grad
    direction = moment_one / first_fix / (jnp.sqrt(moment_two / second_fix) + adam_eps)
    new_master = gate_master - learn_rate * (direction + weight_decay * gate_master)
    new_weights = new_master.astype(jnp.bfloat16)
    flat_grad = slot_grad.reshape(EXPERTS * rows_all, D)
    flat_score = slot_score.reshape(EXPERTS * rows_all)
    blocks = N_EP * N_DP

    def per_block(packed):
        block, experts, slots, shared = packed
        source = block // N_DP
        group = block % N_DP
        served = (experts < EXPERTS) & (slots < CAP)
        target = ((experts * N_DP + group) * N_EP + source) * CAP + slots
        target = jnp.where(served, target, jnp.zeros_like(target)).astype(jnp.int32)
        picked = jnp.take(flat_grad, target, axis=0).astype(jnp.float32)
        routed = lax.optimization_barrier(jnp.sum(jnp.where(served[:, :, None], picked, jnp.float32(0.0)), axis=1))
        grad_block = (shared.astype(jnp.float32) + routed).astype(jnp.bfloat16)
        score_block = jnp.where(served, jnp.take(flat_score, target).astype(jnp.float32), jnp.float32(0.0)).astype(jnp.bfloat16)
        return (grad_block, score_block)
    grad_input, score_grad = lax.map(per_block, (jnp.arange(blocks, dtype=jnp.int32), route_experts.reshape(blocks, TOK_DEV, TOP), route_slots.reshape(blocks, TOK_DEV, TOP), shared_grad.reshape(blocks, TOK_DEV, D)))
    grad_input = grad_input.reshape(TOKENS, D)
    score_grad = score_grad.reshape(TOKENS, TOP)
    return (grad_input, score_grad, new_master, moment_one.astype(jnp.bfloat16), moment_two.astype(jnp.bfloat16), new_weights)
```

```python
import jax
import jax.numpy as jnp
from jax import lax
from jax.experimental import pallas as pl
from jax.experimental.pallas import tpu as pltpu
from jax.sharding import PartitionSpec as P

first_decay = 0.9
second_decay = 0.95
learn_rate = 0.001
weight_decay = 0.1
adam_eps = 1e-08
first_fix = 1.0 - 0.9**10
second_fix = 1.0 - 0.95**10

D = 2560
H = 768
CAP = 24
EP = 16
DP = 16
ROWS = EP * CAP
TOK = 256
TOP = 6
BLK = D // DP
CHUNK = 640
NCH = D // CHUNK
MESH = pl.DeviceIdType.MESH
F32 = jnp.float32
BF16 = jnp.bfloat16


def kernel(
    re_h, rs_h, sh_h, cnt_h, xin_h, g_h, u_h, e_h, prob_h, mst_h, fst_h, snd_h, up_h,
    gi_o, sc_o, nm_o, nf_o, ns_o, nw_o,
    re, rs, cnt, prob, xin, g_in, u_in, e_in, mst, fst, snd, shared,
    w_all, dgate, dup, sc_row, sc_tile, sc_recv, comb,
    tmp, keep, r1_send, r1_recv, r2_send, r2_recv, r3_send, r3_recv, total,
    sg, rg, gi_v, sc_v, nm_v, nf_v, ns_v, nw_v,
    in_sem, out_sem, ag_s, ag_r, a2_s, a2_r, sc_s, sc_r, r1_s, r1_r, r2_s, r2_r, r3_s, r3_r,
    ng_s, ng_r,
):
    ep = lax.axis_index("ep")
    dp = lax.axis_index("dp")
    y, x, k = dp // 8, lax.rem(dp // 2, 4), lax.rem(dp, 2)

    def at(yy, xx, kk):
        return yy * 8 + lax.rem(xx + 4, 4) * 2 + kk

    sib, yp, xr, xl, x2 = at(y, x, 1 - k), at(1 - y, x, k), at(y, x + 1, k), at(y, x - 1, k), at(y, x + 2, k)

    def remote(src, dst, s, r, dst_dp):
        return pltpu.make_async_remote_copy(
            src_ref=src, dst_ref=dst, send_sem=s, recv_sem=r,
            device_id=(ep, dst_dp), device_id_type=MESH)

    loads = []

    def load(src, dst):
        c = pltpu.make_async_copy(src, dst, in_sem.at[len(loads)])
        c.start()
        loads.append(c)
        return c

    l_mst = load(mst_h.at[0], mst)
    l_up = load(up_h.at[0], w_all.at[dp, 1])
    l_g = load(g_h.at[0], g_in)
    l_u = load(u_h.at[0], u_in)
    l_e = load(e_h.at[0], e_in)
    l_cnt = load(cnt_h, cnt)
    l_prob = load(prob_h, prob)
    l_x = load(xin_h.at[0], xin)
    l_re = load(re_h, re)
    l_rs = load(rs_h, rs)
    l_sh = load(sh_h, shared)
    l_f = load(fst_h.at[0], fst)
    l_s = load(snd_h.at[0], snd)

    bar = pltpu.get_barrier_semaphore()
    for peer in (sib, yp, xr, xl, x2):
        pl.semaphore_signal(bar, inc=1, device_id=(ep, peer), device_id_type=MESH)

    def greet(i, _):
        pl.semaphore_signal(bar, inc=1, device_id=(lax.rem(ep + i, EP), dp), device_id_type=MESH)
        return _

    lax.fori_loop(1, EP, greet, 0)

    l_mst.wait()
    for r in range(0, BLK, 32):
        w_all[dp, 0, pl.ds(r, 32), :] = mst[pl.ds(r, 32), :].astype(BF16)
    l_up.wait()
    pl.semaphore_wait(bar, 5 + EP - 1)

    def ag(op, slot, half, to):
        ref = w_all.at[slot] if half is None else w_all.at[slot, half]
        return remote(ref, ref, ag_s.at[op], ag_r.at[op], to)

    plan = {
        0: (dp, None, sib), 1: (dp, None, yp), 2: (dp, None, xr), 3: (dp, None, xl),
        4: (xl, 0, xr), 5: (xl, None, sib), 6: (xr, 1, xl), 7: (xr, None, sib),
        8: (yp, None, xr), 9: (yp, None, xl), 10: (yp, None, sib),
        11: (at(1 - y, x - 1, k), 0, xr), 12: (at(1 - y, x - 1, k), None, sib),
        13: (at(1 - y, x + 1, k), 1, xl), 14: (at(1 - y, x + 1, k), None, sib),
        15: (x2, None, sib), 16: (at(1 - y, x + 2, k), None, sib),
    }
    def ag_go(*ops):
        for op in ops:
            ag(op, *plan[op]).start()

    def ag_wait(*ops):
        for op in ops:
            half = plan[op][1]
            ref = w_all.at[dp] if half is None else w_all.at[dp, half]
            remote(ref, ref, ag_s.at[op], ag_r.at[op], sib).wait_recv()

    ag_go(2, 3, 1, 0)

    l_g.wait()
    l_u.wait()
    l_e.wait()
    l_cnt.wait()
    l_prob.wait()
    TILE = 2 * CAP

    def hidden(i, carry):
        rows = pl.ds(pl.multiple_of(i * TILE, TILE), TILE)
        gv = g_in[rows, :].astype(F32)
        uv = u_in[rows, :].astype(F32)
        ev = e_in[rows, :].astype(F32)
        row = lax.broadcasted_iota(jnp.int32, (TILE, ROWS), 0) + i * TILE
        lane = lax.broadcasted_iota(jnp.int32, (TILE, ROWS), 1)
        p = jnp.sum(jnp.where(row == lane, prob[...], 0.0), axis=1, keepdims=True)
        row16 = lax.broadcasted_iota(jnp.int32, (TILE, EP), 0)
        second = (row16 >= CAP).astype(jnp.int32)
        block16 = second + 2 * i
        lane16 = lax.broadcasted_iota(jnp.int32, (TILE, EP), 1)
        limit = jnp.sum(jnp.where(block16 == lane16, cnt[...], 0), axis=1, keepdims=True)
        rank = (row16 - CAP * second)[:, :1]
        live = rank < limit
        sg_ = jax.nn.sigmoid(gv)
        act = gv * sg_
        score = jnp.sum(ev * act * uv, axis=1, keepdims=True)
        pe = p * ev
        d_up = (pe * act).astype(BF16)
        d_gate = (pe * uv * sg_ * (1.0 + gv * (1.0 - sg_))).astype(BF16)
        zero = jnp.zeros_like(d_up)
        dup[rows, :] = jnp.where(live, d_up, zero)
        dgate[rows, :] = jnp.where(live, d_gate, zero)
        score = score.astype(BF16).astype(F32)
        lane128 = lax.broadcasted_iota(jnp.int32, (TILE, 128), 1)
        spread = jnp.where(lane128 == rank, score, 0.0)
        sc_row[pl.ds(2 * i, 1), :] = jnp.sum(spread[:CAP], axis=0, keepdims=True)
        sc_row[pl.ds(2 * i + 1, 1), :] = jnp.sum(spread[CAP:], axis=0, keepdims=True)
        return carry

    lax.fori_loop(0, ROWS // TILE, hidden, 0)
    sc_tile[...] = sc_row[...].astype(BF16)

    def sc_copy(i):
        to = lax.rem(ep + i, EP)
        return pltpu.make_async_remote_copy(
            src_ref=sc_tile, dst_ref=sc_recv.at[ep], send_sem=sc_s.at[i], recv_sem=sc_r.at[i],
            device_id=(to, dp), device_id_type=MESH)

    sc_recv[ep] = sc_tile[...]

    l_x.wait()

    def r1_copy(c):
        blocks = pl.ds(pl.multiple_of(2 * c, 2), 2)
        return remote(r1_send.at[blocks], r1_recv.at[blocks], r1_s.at[c], r1_r.at[c], sib)

    def weight_part(i, carry):
        c = lax.rem(2 * (1 - y) + i, NCH)
        cols = pl.ds(pl.multiple_of(c * CHUNK, CHUNK), CHUNK)
        part = lax.dot_general(
            xin[:, cols], dgate[...], (((0,), (0,)), ((), ())), preferred_element_type=F32)
        tmp[...] = part.reshape(4, BLK, H)
        for j in range(2):
            keep[2 * c + j] = tmp[2 * j + k]
            r1_send[2 * c + j] = tmp[2 * j + 1 - k]
        r1_copy(c).start()
        return carry

    lax.fori_loop(0, NCH, weight_part, 0)

    def a2_copy(i, n):
        to = lax.rem(ep + n, EP)
        return pltpu.make_async_remote_copy(
            src_ref=sg.at[i, to], dst_ref=rg.at[i, ep], send_sem=a2_s.at[i, n], recv_sem=a2_r.at[i, n],
            device_id=(to, dp), device_id_type=MESH)

    pair = x // 2
    order = (2 * y + pair, 2 * y + 1 - pair, 2 * (1 - y) + pair, 2 * (1 - y) + 1 - pair)

    def rows_out(i):
        q = order[i]
        blocks = pl.ds(pl.multiple_of(4 * q, 4), 4)
        dims = (((1,), (1,)), ((), ()))
        wg = w_all[blocks, 0].reshape(CHUNK, H)
        wu = w_all[blocks, 1].reshape(CHUNK, H)
        out = lax.dot_general(dgate[...], wg, dims, preferred_element_type=F32)
        out = out + lax.dot_general(dup[...], wu, dims, preferred_element_type=F32)
        sg[i] = out.reshape(EP, CAP, CHUNK).astype(BF16)

        def send(n, carry):
            a2_copy(i, n).start()
            return carry

        lax.fori_loop(1, EP, send, 0)
        rg[i, ep] = sg[i, ep]

    ag_wait(2, 3)
    ag_go(4, 6, 5, 7)
    ag_wait(1)
    ag_go(8, 9, 10)
    ag_wait(0, 5, 7)
    rows_out(0)

    def send_scores(n, carry):
        sc_copy(n).start()
        return carry

    lax.fori_loop(1, EP, send_scores, 0)

    def r2_copy():
        return remote(r2_send, r2_recv, r2_s, r2_r, yp)

    def r1_wait(i, carry):
        c = lax.rem(2 * (1 - y) + i, NCH)
        r1_copy(c).wait_recv()
        return carry

    lax.fori_loop(0, 2, r1_wait, 0)

    def to_partner(n, carry):
        c = 4 * (1 - y) + n
        r2_send[n] = (keep[c] + r1_recv[c]).astype(BF16)
        return carry

    lax.fori_loop(0, 4, to_partner, 0)
    r2_copy().start()

    ag_wait(4, 6)
    ag_go(15)
    ag_wait(15)
    rows_out(1)

    ag_wait(8, 9)
    ag_go(11, 13, 12, 14)
    ag_wait(10, 12, 14)
    rows_out(2)

    lax.fori_loop(2, 4, r1_wait, 0)
    r2_copy().wait_recv()

    def r3_copy(n, to):
        return remote(r3_send.at[n], r3_recv.at[n], r3_s.at[n], r3_r.at[n], to)

    hops = (xr, xl, x2)
    for n, dx in enumerate((1, 3, 2)):
        xx = lax.rem(x + dx, 4)
        c = 4 * y + xx
        r3_send[n] = (keep[c] + r1_recv[c] + r2_recv[xx].astype(F32)).astype(BF16)
        r3_copy(n, hops[n]).start()
    total[...] = keep[4 * y + x] + r1_recv[4 * y + x] + r2_recv[x].astype(F32)

    ag_wait(11, 13)
    ag_go(16)
    ag_wait(16)
    rows_out(3)

    l_f.wait()
    l_s.wait()
    for n in range(3):
        r3_copy(n, hops[n]).wait_recv()

    def adam(i, carry):
        rows = pl.ds(pl.multiple_of(i * 32, 32), 32)
        wg = total[rows, :]
        for n in range(3):
            wg = wg + r3_recv[n, rows, :].astype(F32)
        m1 = first_decay * fst[rows, :].astype(F32) + (1.0 - first_decay) * wg
        m2 = second_decay * snd[rows, :].astype(F32) + (1.0 - second_decay) * wg * wg
        direction = m1 / first_fix / (jnp.sqrt(m2 / second_fix) + adam_eps)
        now = mst[rows, :]
        new = now - learn_rate * (direction + weight_decay * now)
        nm_v[rows, :] = new
        nf_v[rows, :] = m1.astype(BF16)
        ns_v[rows, :] = m2.astype(BF16)
        nw_v[rows, :] = new.astype(BF16)
        return carry

    lax.fori_loop(0, BLK // 32, adam, 0)

    outs = []

    def store(src, dst):
        c = pltpu.make_async_copy(src, dst, out_sem.at[len(outs)])
        c.start()
        outs.append(c)

    def nw_ref(slot, half=None):
        if half is None:
            return nw_o.at[0, pl.ds(pl.multiple_of(slot * BLK, BLK), BLK)]
        return nw_o.at[0, pl.ds(pl.multiple_of(slot * BLK + half * (BLK // 2), BLK // 2), BLK // 2)]

    def ng(op):
        slot, half, to = plan[op]
        ref = nw_ref(slot, half)
        return remote(nw_v if op < 4 else ref, ref, ng_s.at[op], ng_r.at[op], to)

    def ng_go(*ops):
        for op in ops:
            ng(op).start()

    def ng_wait(*ops):
        for op in ops:
            ng(op).wait_recv()

    ng_go(2, 3, 1, 0)
    store(nw_v, nw_ref(dp))
    store(nm_v, nm_o.at[0])
    store(nf_v, nf_o.at[0])
    store(ns_v, ns_o.at[0])

    l_re.wait()
    l_rs.wait()
    rank_of = rs[...]
    expert_of = re[...]
    served = (expert_of < EP) & (rank_of < CAP)
    target = jnp.where(served, expert_of * CAP + rank_of, -1)
    lane = lax.broadcasted_iota(jnp.int32, (TOK, ROWS), 1)
    hits = jnp.zeros((TOK, ROWS), F32)
    for j in range(TOP):
        hits = hits + jnp.where(target[:, j:j + 1] == lane, 1.0, 0.0)
    comb[...] = hits.astype(BF16)

    l_sh.wait()

    def tokens(i):
        def got(n, carry):
            a2_copy(i, n).wait_recv()
            return carry

        lax.fori_loop(1, EP, got, 0)
        rows = rg[i].astype(F32).reshape(ROWS, CHUNK).astype(BF16)
        routed = jnp.dot(comb[...], rows, preferred_element_type=F32)
        cols = pl.ds(pl.multiple_of(order[i] * CHUNK, CHUNK), CHUNK)
        gi_v[:, cols] = (shared[:, cols].astype(F32) + routed).astype(BF16)
        store(gi_v.at[:, cols], gi_o.at[:, cols])

    tokens(0)
    ng_wait(2, 3)
    ng_go(4, 6, 5, 7)
    ng_wait(1)
    ng_go(8, 9, 10)
    tokens(1)

    def got_score(n, carry):
        sc_copy(n).wait_recv()
        return carry

    lax.fori_loop(1, EP, got_score, 0)
    source = lax.broadcasted_iota(jnp.int32, (EP, EP, 128), 1)
    mine = jnp.sum(jnp.where(source == ep, sc_recv[...].astype(F32), 0.0), axis=1).astype(BF16)
    lane_e = lax.broadcasted_iota(jnp.int32, (TOK, EP), 1)
    lane_q = lax.broadcasted_iota(jnp.int32, (TOK, 128), 1)
    result = jnp.zeros((TOK, 128), F32)
    for j in range(TOP):
        pick = jnp.where(expert_of[:, j:j + 1] == lane_e, 1.0, 0.0).astype(BF16)
        scores = jnp.dot(pick, mine, preferred_element_type=F32)
        hit = (rank_of[:, j:j + 1] == lane_q) & served[:, j:j + 1]
        value = jnp.sum(jnp.where(hit, scores, 0.0), axis=1, keepdims=True)
        result = jnp.where(lane_q == j, value, result)
    sc_v[...] = result[:, :TOP].astype(BF16)
    store(sc_v, sc_o)

    ng_wait(4, 6)
    ng_go(15)
    ng_wait(8, 9)
    ng_go(11, 13, 12, 14)
    tokens(2)
    ng_wait(11, 13)
    ng_go(16)
    tokens(3)

    ng_wait(0, 5, 7, 10, 12, 14, 15, 16)
    for op in range(17):
        ag(op, *plan[op]).wait_send()
        ng(op).wait_send()

    def sent(n, carry):
        for i in range(NCH):
            a2_copy(i, n).wait_send()
        sc_copy(n).wait_send()
        return carry

    lax.fori_loop(1, EP, sent, 0)
    for c in range(NCH):
        r1_copy(c).wait_send()
    r2_copy().wait_send()
    for n in range(3):
        r3_copy(n, hops[n]).wait_send()
    for c in outs:
        c.wait()


def per_device(*args):
    any_spec = pl.BlockSpec(memory_space=pl.ANY)
    dma = pltpu.SemaphoreType.DMA
    V = pltpu.VMEM
    scratch = [
        V((TOK, TOP), jnp.int32), V((TOK, TOP), jnp.int32), V((1, EP), jnp.int32), V((1, ROWS), F32),
        V((ROWS, D), BF16), V((ROWS, H), BF16), V((ROWS, H), BF16), V((ROWS, H), BF16),
        V((BLK, H), F32), V((BLK, H), BF16), V((BLK, H), BF16), V((TOK, D), BF16),
        V((DP, 2, BLK, H), BF16), V((ROWS, H), BF16), V((ROWS, H), BF16),
        V((EP, 128), F32), V((EP, 128), BF16), V((EP, EP, 128), BF16), V((TOK, ROWS), BF16),
        V((4, BLK, H), F32), V((8, BLK, H), F32), V((8, BLK, H), F32), V((8, BLK, H), F32),
        V((4, BLK, H), BF16), V((4, BLK, H), BF16), V((3, BLK, H), BF16), V((3, BLK, H), BF16),
        V((BLK, H), F32),
        V((NCH, EP, CAP, CHUNK), BF16), V((NCH, EP, CAP, CHUNK), BF16),
        V((TOK, D), BF16), V((TOK, TOP), BF16), V((BLK, H), F32), V((BLK, H), BF16),
        V((BLK, H), BF16), V((BLK, H), BF16),
        dma((13,)), dma((9,)), dma((17,)), dma((17,)), dma((NCH, EP)), dma((NCH, EP)),
        dma((EP,)), dma((EP,)), dma((NCH,)), dma((NCH,)), dma, dma, dma((3,)), dma((3,)),
        dma((17,)), dma((17,)),
    ]
    return pl.pallas_call(
        kernel,
        out_shape=[
            jax.ShapeDtypeStruct((TOK, D), BF16), jax.ShapeDtypeStruct((TOK, TOP), BF16),
            jax.ShapeDtypeStruct((1, BLK, H), F32), jax.ShapeDtypeStruct((1, BLK, H), BF16),
            jax.ShapeDtypeStruct((1, BLK, H), BF16), jax.ShapeDtypeStruct((1, D, H), BF16),
        ],
        in_specs=[any_spec] * 13,
        out_specs=[any_spec] * 6,
        scratch_shapes=scratch,
        compiler_params=pltpu.CompilerParams(
            collective_id=0, has_side_effects=True, vmem_limit_bytes=60 * 2**20),
        name="backward_tail",
    )(*args)


def solution(mesh):
    in_specs = (
        P(("ep", "dp"), None),
        P(("ep", "dp"), None),
        P(("ep", "dp"), None),
        P("ep", "dp"),
        P("ep", "dp", None),
        P("ep", "dp", None),
        P("ep", "dp", None),
        P("ep", "dp", None),
        P("ep", "dp"),
        P("ep", "dp", None),
        P("ep", "dp", None),
        P("ep", "dp", None),
        P("ep", "dp", None),
    )
    out_specs = (
        P(("ep", "dp"), None),
        P(("ep", "dp"), None),
        P("ep", "dp", None),
        P("ep", "dp", None),
        P("ep", "dp", None),
        P("ep", None, None),
    )
    return jax.shard_map(
        per_device, mesh=mesh, in_specs=in_specs, out_specs=out_specs, check_vma=False
    )
```

```python
import jax
import jax.numpy as jnp
from jax import lax
from jax.experimental import pallas as pl
from jax.experimental.pallas import tpu as pltpu
from jax.sharding import PartitionSpec as P

first_decay = 0.9
second_decay = 0.95
learn_rate = 0.001
weight_decay = 0.1
adam_eps = 1e-08
first_fix = 1.0 - 0.9**10
second_fix = 1.0 - 0.95**10

D = 2560
H = 768
CAP = 24
EP = 16
DP = 16
ROWS = EP * CAP
TOK = 256
TOP = 6
BLK = D // DP
CHUNK = 640
NCH = D // CHUNK
MESH = pl.DeviceIdType.MESH
F32 = jnp.float32
BF16 = jnp.bfloat16


PIECES = ((0, 80), (80, 80))
NQ = len(PIECES)


def kernel(
    re_h, rs_h, sh_h, cnt_h, xin_h, g_h, u_h, e_h, prob_h, mst_h, fst_h, snd_h, up_h,
    gi_o, sc_o, nm_o, nf_o, ns_o, nw_o,
    re, rs, cnt, prob, xin, g_in, u_in, e_in, mst, fst, snd, shared,
    w_gate, w_up, dgate, dup, sc_row, sc_tile, sc_recv, comb,
    tmp, keep, r1_send, r1_recv, r2_send, r2_recv, r3_send, r3_recv,
    sg_a, rg_a, sg_b, rg_b, sg, rg, gi_v, sc_v, nm_v, nf_v, ns_v, nw_v,
    in_sem, out_sem, ag_s, ag_r, a2_s, a2_r, sc_s, sc_r, r1_s, r1_r, r2_s, r2_r, r3_s, r3_r,
    ng_s, ng_r,
):
    ep = lax.axis_index("ep")
    dp = lax.axis_index("dp")
    y, x, k = dp // 8, lax.rem(dp // 2, 4), lax.rem(dp, 2)

    def at(yy, xx, kk):
        return yy * 8 + lax.rem(xx + 4, 4) * 2 + kk

    sib, yp, xr, xl, x2 = at(y, x, 1 - k), at(1 - y, x, k), at(y, x + 1, k), at(y, x - 1, k), at(y, x + 2, k)
    yxr, yxl, yx2 = at(1 - y, x + 1, k), at(1 - y, x - 1, k), at(1 - y, x + 2, k)

    def remote(src, dst, s, r, dst_dp):
        return pltpu.make_async_remote_copy(
            src_ref=src, dst_ref=dst, send_sem=s, recv_sem=r,
            device_id=(ep, dst_dp), device_id_type=MESH)

    def rows_of(slot, q=None):
        if q is None:
            return pl.ds(pl.multiple_of(slot * BLK, BLK), BLK)
        return pl.ds(pl.multiple_of(slot * BLK + PIECES[q][0], 16), PIECES[q][1])

    loads = []

    def load(src, dst):
        c = pltpu.make_async_copy(src, dst, in_sem.at[len(loads)])
        c.start()
        loads.append(c)
        return c

    l_mst = load(mst_h.at[0], mst)
    l_up = load(up_h.at[0], w_up.at[rows_of(dp)])
    l_g = load(g_h.at[0], g_in)
    l_u = load(u_h.at[0], u_in)
    l_e = load(e_h.at[0], e_in)
    l_cnt = load(cnt_h, cnt)
    l_prob = load(prob_h, prob)
    l_x = load(xin_h.at[0], xin)
    l_re = load(re_h, re)
    l_rs = load(rs_h, rs)
    l_f = load(fst_h.at[0], fst)
    l_s = load(snd_h.at[0], snd)
    l_sh = load(sh_h, shared)

    bar = pltpu.get_barrier_semaphore()
    for peer in (sib, yp, xr, xl, x2):
        pl.semaphore_signal(bar, inc=1, device_id=(ep, peer), device_id_type=MESH)

    def greet(i, _):
        pl.semaphore_signal(bar, inc=1, device_id=(lax.rem(ep + i, EP), dp), device_id_type=MESH)
        return _

    lax.fori_loop(1, EP, greet, 0)

    l_mst.wait()
    for r in range(0, BLK, 32):
        w_gate[pl.ds(pl.multiple_of(dp * BLK + r, 32), 32), :] = mst[pl.ds(r, 32), :].astype(BF16)
    l_up.wait()
    pl.semaphore_wait(bar, 5 + EP - 1)

    plan = (
        (dp, 0, xr), (dp, 1, xr), (dp, 1, xl), (dp, 0, xl),
        (dp, 0, yp), (dp, 1, yp), (dp, 0, sib), (dp, 1, sib),
        (xl, 0, xr), (xr, 1, xl),
        (xl, 0, sib), (xl, 1, sib), (xr, 0, sib), (xr, 1, sib),
        (yp, 0, xr), (yp, 0, xl), (yp, 1, xr), (yp, 1, xl), (yp, 0, sib), (yp, 1, sib),
        (yxl, 0, xr), (yxr, 1, xl),
        (yxl, 0, sib), (yxl, 1, sib), (yxr, 0, sib), (yxr, 1, sib),
        (x2, 0, sib), (x2, 1, sib), (yx2, 0, sib), (yx2, 1, sib),
    )

    def ag(op):
        slot, piece, to = plan[op]
        ref = (w_gate, w_up)[piece].at[rows_of(slot)]
        return remote(ref, ref, ag_s.at[op], ag_r.at[op], to)

    def ag_go(*ops):
        for op in ops:
            ag(op).start()

    def ag_wait(*ops):
        for op in ops:
            ag(op).wait_recv()

    ag_go(0, 2, 4, 1, 3, 5, 6, 7)

    l_g.wait()
    l_u.wait()
    l_e.wait()
    l_cnt.wait()
    l_prob.wait()
    TILE = 2 * CAP

    def hidden(i, carry):
        rows = pl.ds(pl.multiple_of(i * TILE, TILE), TILE)
        gv = g_in[rows, :].astype(F32)
        uv = u_in[rows, :].astype(F32)
        ev = e_in[rows, :].astype(F32)
        row = lax.broadcasted_iota(jnp.int32, (TILE, ROWS), 0) + i * TILE
        lane = lax.broadcasted_iota(jnp.int32, (TILE, ROWS), 1)
        p = jnp.sum(jnp.where(row == lane, prob[...], 0.0), axis=1, keepdims=True)
        row16 = lax.broadcasted_iota(jnp.int32, (TILE, EP), 0)
        second = (row16 >= CAP).astype(jnp.int32)
        block16 = second + 2 * i
        lane16 = lax.broadcasted_iota(jnp.int32, (TILE, EP), 1)
        limit = jnp.sum(jnp.where(block16 == lane16, cnt[...], 0), axis=1, keepdims=True)
        rank = (row16 - CAP * second)[:, :1]
        live = rank < limit
        sg_ = jax.nn.sigmoid(gv)
        act = gv * sg_
        score = jnp.sum(ev * act * uv, axis=1, keepdims=True)
        pe = p * ev
        d_up = (pe * act).astype(BF16)
        d_gate = (pe * uv * sg_ * (1.0 + gv * (1.0 - sg_))).astype(BF16)
        zero = jnp.zeros_like(d_up)
        dup[rows, :] = jnp.where(live, d_up, zero)
        dgate[rows, :] = jnp.where(live, d_gate, zero)
        score = score.astype(BF16).astype(F32)
        lane128 = lax.broadcasted_iota(jnp.int32, (TILE, 128), 1)
        spread = jnp.where(lane128 == rank, score, 0.0)
        sc_row[pl.ds(2 * i, 1), :] = jnp.sum(spread[:CAP], axis=0, keepdims=True)
        sc_row[pl.ds(2 * i + 1, 1), :] = jnp.sum(spread[CAP:], axis=0, keepdims=True)
        return carry

    lax.fori_loop(0, ROWS // TILE, hidden, 0)
    sc_tile[...] = sc_row[...].astype(BF16)

    def sc_copy(i):
        to = lax.rem(ep + i, EP)
        return pltpu.make_async_remote_copy(
            src_ref=sc_tile, dst_ref=sc_recv.at[ep], send_sem=sc_s.at[i], recv_sem=sc_r.at[i],
            device_id=(to, dp), device_id_type=MESH)

    sc_recv[ep] = sc_tile[...]

    pair, odd = x // 2, lax.rem(x, 2)
    base = CHUNK * (2 * y + pair)
    groups = (
        (sg_a, rg_a, base + odd * 384, 256),
        (sg_b, rg_b, base + (1 - odd) * 256, 384),
        (sg.at[0], rg.at[0], CHUNK * (2 * y + 1 - pair), CHUNK),
        (sg.at[1], rg.at[1], CHUNK * (2 * (1 - y) + pair), CHUNK),
        (sg.at[2], rg.at[2], CHUNK * (2 * (1 - y) + 1 - pair), CHUNK),
    )

    def a2_copy(i, n):
        to = lax.rem(ep + n, EP)
        src, dst = groups[i][:2]
        return pltpu.make_async_remote_copy(
            src_ref=src.at[to], dst_ref=dst.at[ep], send_sem=a2_s.at[i, n], recv_sem=a2_r.at[i, n],
            device_id=(to, dp), device_id_type=MESH)

    def rows_send(i, first, last, odd_step):
        def send(n, carry):
            a2_copy(i, 2 * n + odd_step).start()
            return carry

        lax.fori_loop(first, last, send, 0)

    def rows_out(i, later=False):
        src, dst, col, width = groups[i]
        rows = pl.ds(pl.multiple_of(col, 128), width)
        dims = (((1,), (1,)), ((), ()))
        out = lax.dot_general(dgate[...], w_gate[rows, :], dims, preferred_element_type=F32)
        out = out + lax.dot_general(dup[...], w_up[rows, :], dims, preferred_element_type=F32)
        src[...] = out.reshape(EP, CAP, width).astype(BF16)

        dst[ep] = src[ep]
        rows_send(i, 1, EP // 2, 0)
        if not later:
            rows_send(i, 0, EP // 2, 1)

    l_x.wait()

    def r1_copy(c):
        blocks = pl.ds(pl.multiple_of(2 * c, 2), 2)
        return remote(r1_send.at[blocks], r1_recv.at[blocks], r1_s.at[c], r1_r.at[c], sib)

    def weight_part(i, carry):
        c = lax.rem(2 * (1 - y) + i, NCH)
        cols = pl.ds(pl.multiple_of(c * CHUNK, CHUNK), CHUNK)
        part = lax.dot_general(
            xin[:, cols], dgate[...], (((0,), (0,)), ((), ())), preferred_element_type=F32)
        tmp[...] = part.reshape(4, BLK, H)
        for j in range(2):
            keep[2 * c + j] = tmp[2 * j + k]
            r1_send[2 * c + j] = tmp[2 * j + 1 - k]
        r1_copy(c).start()
        return carry

    def r1_wait(i, carry):
        c = lax.rem(2 * (1 - y) + i, NCH)
        r1_copy(c).wait_recv()
        return carry

    def piece_of(q):
        return pl.ds(*PIECES[q])

    def r2_copy(q):
        rows = piece_of(q)
        return remote(r2_send.at[:, rows], r2_recv.at[:, rows], r2_s.at[q], r2_r.at[q], yp)

    lax.fori_loop(0, 2, weight_part, 0)
    ag_wait(6, 7)
    rows_out(0, later=True)
    lax.fori_loop(2, NCH, weight_part, 0)
    ag_wait(0, 2)
    ag_go(8, 9, 10, 13)
    ag_wait(4)
    ag_go(14, 15, 18)

    lax.fori_loop(0, 2, r1_wait, 0)
    for q in range(NQ):
        rows = piece_of(q)

        def to_partner(n, carry):
            c = 4 * (1 - y) + n
            r2_send[n, rows] = (keep[c, rows] + r1_recv[c, rows]).astype(BF16)
            return carry

        lax.fori_loop(0, 4, to_partner, 0)
        r2_copy(q).start()

    def send_scores(n, carry):
        sc_copy(n).start()
        return carry

    lax.fori_loop(1, EP, send_scores, 0)

    l_re.wait()
    l_rs.wait()
    rank_of = rs[...]
    expert_of = re[...]
    served = (expert_of < EP) & (rank_of < CAP)
    target = jnp.where(served, expert_of * CAP + rank_of, -1)
    row_j = lax.broadcasted_iota(jnp.int32, (ROWS, TOK), 0)
    hits = jnp.zeros((ROWS, TOK), F32)
    for j in range(TOP):
        hits = hits + jnp.where(target[j:j + 1, :] == row_j, 1.0, 0.0)
    comb[...] = hits.T.astype(BF16)

    ag_wait(1, 3)
    ag_go(11, 12)
    ag_wait(5)
    ag_go(16, 17, 19)
    ag_wait(10, 11, 12, 13)
    rows_out(1, later=True)

    def r3_copy(n, q):
        rows = piece_of(q)
        return remote(r3_send.at[n, rows], r3_recv.at[n, rows], r3_s.at[n, q], r3_r.at[n, q],
                      (xr, xl, x2)[n])

    def over_x(q):
        r2_copy(q).wait_recv()
        rows = piece_of(q)
        for n, dx in enumerate((1, 3, 2)):
            xx = lax.rem(x + dx, 4)
            c = 4 * y + xx
            r3_send[n, rows] = (
                keep[c, rows] + r1_recv[c, rows] + r2_recv[xx, rows].astype(F32)
            ).astype(BF16)
            r3_copy(n, q).start()

    outs = []

    def store(src, dst):
        c = pltpu.make_async_copy(src, dst, out_sem.at[len(outs)])
        c.start()
        outs.append(c)

    ng_plan = (
        (dp, 0, xr), (dp, 0, xl), (dp, 0, yp), (dp, 0, sib),
        (xl, 0, xr), (xl, 0, sib), (xr, 0, sib),
        (yp, 0, xr), (yp, 0, xl), (yp, 0, sib),
        (yxr, 0, xl), (yxl, 0, sib), (yxr, 0, sib), (x2, 0, sib), (yx2, 0, sib),
        (dp, 1, xr), (dp, 1, xl), (dp, 1, yp), (dp, 1, sib),
        (xr, 1, xl), (xr, 1, yp), (xr, 1, sib), (xl, 1, yp), (xl, 1, sib),
        (x2, 1, yp), (x2, 1, sib), (yp, 1, sib), (yxr, 1, sib), (yxl, 1, sib), (yx2, 1, sib),
    )

    def ng(op):
        slot, q, to = ng_plan[op]
        ref = nw_o.at[0, rows_of(slot, q)]
        src = nw_v.at[piece_of(q)] if slot is dp else ref
        return remote(src, ref, ng_s.at[op], ng_r.at[op], to)

    def ng_go(*ops):
        for op in ops:
            ng(op).start()

    def ng_hop(*moves):
        for arrived, *onward in moves:
            ng(arrived).wait_recv()
            ng_go(*onward)

    def step(q):
        for n in range(3):
            r3_copy(n, q).wait_recv()
        first, size = PIECES[q]

        def adam(i, carry):
            rows = pl.ds(pl.multiple_of(first + i * 16, 16), 16)
            own = 4 * y + x
            wg = keep[own, rows] + r1_recv[own, rows] + r2_recv[x, rows].astype(F32)
            for n in range(3):
                wg = wg + r3_recv[n, rows].astype(F32)
            m1 = first_decay * fst[rows, :].astype(F32) + (1.0 - first_decay) * wg
            m2 = second_decay * snd[rows, :].astype(F32) + (1.0 - second_decay) * wg * wg
            direction = m1 / first_fix / (jnp.sqrt(m2 / second_fix) + adam_eps)
            now = mst[rows, :]
            new = now - learn_rate * (direction + weight_decay * now)
            nm_v[rows, :] = new
            nf_v[rows, :] = m1.astype(BF16)
            ns_v[rows, :] = m2.astype(BF16)
            nw_v[rows, :] = new.astype(BF16)
            return carry

        lax.fori_loop(0, size // 16, adam, 0)

    def tokens(i):
        _, got, col, width = groups[i]

        def arrived(n, carry):
            a2_copy(i, n).wait_recv()
            return carry

        lax.fori_loop(1, EP, arrived, 0)
        rows = got[...].astype(F32).reshape(ROWS, width).astype(BF16)
        routed = jnp.dot(comb[...], rows, preferred_element_type=F32)
        cols = pl.ds(pl.multiple_of(col, 128), width)
        gi_v[:, cols] = (shared[:, cols].astype(F32) + routed).astype(BF16)
        store(gi_v.at[:, cols], gi_o.at[:, cols])

    def scores_out():
        def got_score(n, carry):
            sc_copy(n).wait_recv()
            return carry

        lax.fori_loop(1, EP, got_score, 0)
        source = lax.broadcasted_iota(jnp.int32, (EP, EP, 128), 1)
        mine = jnp.sum(jnp.where(source == ep, sc_recv[...].astype(F32), 0.0), axis=1).astype(BF16)
        row_e = lax.broadcasted_iota(jnp.int32, (EP, TOK), 0)
        row_q = lax.broadcasted_iota(jnp.int32, (128, TOK), 0)
        row_k = lax.broadcasted_iota(jnp.int32, (8, TOK), 0)
        result = jnp.zeros((8, TOK), F32)
        for j in range(TOP):
            pick = jnp.where(expert_of[j:j + 1, :] == row_e, 1.0, 0.0).astype(BF16)
            scores = lax.dot_general(mine, pick, (((0,), (0,)), ((), ())), preferred_element_type=F32)
            hit = jnp.where(served[j:j + 1, :], rank_of[j:j + 1, :], -1) == row_q
            value = jnp.sum(jnp.where(hit, scores, 0.0), axis=0, keepdims=True)
            result = jnp.where(row_k == j, value, result)
        sc_v[...] = result[:TOP].astype(BF16)
        store(sc_v, sc_o)

    l_f.wait()
    l_s.wait()
    l_sh.wait()
    lax.fori_loop(2, NCH, r1_wait, 0)

    ag_wait(8, 9)
    ag_go(26, 27)
    ag_wait(26, 27)
    rows_out(2)
    ag_wait(14, 15)
    ag_go(20, 22, 24)
    over_x(0)
    ag_wait(16, 17)
    ag_go(21, 23, 25)
    ag_wait(18, 19, 22, 23, 24, 25)
    rows_out(3)
    rows_send(0, 0, EP // 2, 1)
    rows_send(1, 0, EP // 2, 1)
    scores_out()
    ag_wait(20, 21)
    ag_go(28, 29)
    over_x(1)
    ag_wait(28, 29)
    rows_out(4)
    step(0)
    ng_go(0, 1, 2, 3)
    step(1)
    ng_go(15, 16, 17, 18)
    ng_hop((0, 4, 5), (2, 7, 8, 9), (16, 19, 20, 21), (15, 22, 23), (1, 6))
    tokens(0)
    tokens(1)
    ng_hop((8, 10, 12), (19, 24, 25), (7, 11), (4, 13), (17, 26), (20, 27), (22, 28))
    store(nw_v, nw_o.at[0, rows_of(dp)])
    store(nm_v, nm_o.at[0])
    store(nf_v, nf_o.at[0])
    store(ns_v, ns_o.at[0])
    tokens(2)
    ng_hop((10, 14), (24, 29))
    tokens(3)
    tokens(4)
    ng_hop(*((op,) for op in (3, 5, 6, 9, 11, 12, 13, 14, 18, 21, 23, 25, 26, 27, 28, 29)))

    for op in range(len(plan)):
        ag(op).wait_send()
        ng(op).wait_send()

    def sent(n, carry):
        for i in range(len(groups)):
            a2_copy(i, n).wait_send()
        sc_copy(n).wait_send()
        return carry

    lax.fori_loop(1, EP, sent, 0)
    for c in range(NCH):
        r1_copy(c).wait_send()
    for q in range(NQ):
        r2_copy(q).wait_send()
        for n in range(3):
            r3_copy(n, q).wait_send()
    for c in outs:
        c.wait()


def finish(*refs):
    n = (len(refs) - 2) // 3
    srcs, dsts, held, in_sem, out_sem = refs[:n], refs[n:2 * n], refs[2 * n:3 * n], refs[-2], refs[-1]
    ins, outs = [], []
    for src, dst, mid in zip(srcs, dsts, held):
        rows = src.shape[-2]
        parts = 8 if rows == D else 4 if rows == TOK else 1
        for i in range(parts):
            part = pl.ds(i * (rows // parts), rows // parts)
            index = (0, part) if len(src.shape) == 3 else (part,)
            m = len(ins)
            ins.append(pltpu.make_async_copy(src.at[index], mid.at[index], in_sem.at[m]))
            outs.append(pltpu.make_async_copy(mid.at[index], dst.at[index], out_sem.at[m]))
    for c in ins:
        c.start()
    for c, o in zip(ins, outs):
        c.wait()
        o.start()
    for o in outs:
        o.wait()


def per_device(route_experts, route_slots, *args):
    any_spec = pl.BlockSpec(memory_space=pl.ANY)
    dma = pltpu.SemaphoreType.DMA
    V = pltpu.VMEM
    scratch = [
        V((TOP, TOK), jnp.int32), V((TOP, TOK), jnp.int32), V((1, EP), jnp.int32), V((1, ROWS), F32),
        V((ROWS, D), BF16), V((ROWS, H), BF16), V((ROWS, H), BF16), V((ROWS, H), BF16),
        V((BLK, H), F32), V((BLK, H), BF16), V((BLK, H), BF16), V((TOK, D), BF16),
        V((D, H), BF16), V((D, H), BF16), V((ROWS, H), BF16), V((ROWS, H), BF16),
        V((EP, 128), F32), V((EP, 128), BF16), V((EP, EP, 128), BF16), V((TOK, ROWS), BF16),
        V((4, BLK, H), F32), V((8, BLK, H), F32), V((8, BLK, H), F32), V((8, BLK, H), F32),
        V((4, BLK, H), BF16), V((4, BLK, H), BF16), V((3, BLK, H), BF16), V((3, BLK, H), BF16),
        V((EP, CAP, 256), BF16), V((EP, CAP, 256), BF16), V((EP, CAP, 384), BF16), V((EP, CAP, 384), BF16),
        V((3, EP, CAP, CHUNK), BF16), V((3, EP, CAP, CHUNK), BF16),
        V((TOK, D), BF16), V((TOP, TOK), BF16), V((BLK, H), F32), V((BLK, H), BF16),
        V((BLK, H), BF16), V((BLK, H), BF16),
        dma((13,)), dma((10,)), dma((30,)), dma((30,)), dma((5, EP)), dma((5, EP)),
        dma((EP,)), dma((EP,)), dma((NCH,)), dma((NCH,)), dma((NQ,)), dma((NQ,)), dma((3, NQ)), dma((3, NQ)),
        dma((30,)), dma((30,)),
    ]
    shapes = [
        jax.ShapeDtypeStruct((TOK, D), BF16), jax.ShapeDtypeStruct((TOP, TOK), BF16),
        jax.ShapeDtypeStruct((1, BLK, H), F32), jax.ShapeDtypeStruct((1, BLK, H), BF16),
        jax.ShapeDtypeStruct((1, BLK, H), BF16), jax.ShapeDtypeStruct((1, D, H), BF16),
    ]
    parts = pl.pallas_call(
        kernel,
        out_shape=shapes,
        in_specs=[any_spec] * 13,
        out_specs=[any_spec] * 6,
        scratch_shapes=scratch,
        compiler_params=pltpu.CompilerParams(
            collective_id=0, has_side_effects=True, vmem_limit_bytes=60 * 2**20),
        name="backward_tail",
    )(route_experts.T, route_slots.T, *args)
    grad, score, *rest = pl.pallas_call(
        finish,
        out_shape=shapes,
        in_specs=[any_spec] * 6,
        out_specs=[any_spec] * 6,
        scratch_shapes=[V(t.shape, t.dtype) for t in shapes] + [dma((16,)), dma((16,))],
        compiler_params=pltpu.CompilerParams(vmem_limit_bytes=60 * 2**20),
        name="finish",
    )(*parts)
    return (grad, score.T, *rest)


def solution(mesh):
    in_specs = (
        P(("ep", "dp"), None),
        P(("ep", "dp"), None),
        P(("ep", "dp"), None),
        P("ep", "dp"),
        P("ep", "dp", None),
        P("ep", "dp", None),
        P("ep", "dp", None),
        P("ep", "dp", None),
        P("ep", "dp"),
        P("ep", "dp", None),
        P("ep", "dp", None),
        P("ep", "dp", None),
        P("ep", "dp", None),
    )
    out_specs = (
        P(("ep", "dp"), None),
        P(("ep", "dp"), None),
        P("ep", "dp", None),
        P("ep", "dp", None),
        P("ep", "dp", None),
        P("ep", None, None),
    )
    return jax.shard_map(
        per_device, mesh=mesh, in_specs=in_specs, out_specs=out_specs, check_vma=False
    )
```

```python
import jax
import jax.numpy as jnp
from jax import lax
from jax.experimental import pallas as pl
from jax.experimental.pallas import tpu as pltpu
from jax.sharding import PartitionSpec as P

first_decay = 0.9
second_decay = 0.95
learn_rate = 0.001
weight_decay = 0.1
adam_eps = 1e-08
first_fix = 1.0 - 0.9**10
second_fix = 1.0 - 0.95**10

D = 2560
H = 768
CAP = 24
EP = 16
DP = 16
ROWS = EP * CAP
TOK = 256
TOP = 6
BLK = D // DP
CHUNK = 640
NCH = D // CHUNK
MESH = pl.DeviceIdType.MESH
F32 = jnp.float32
BF16 = jnp.bfloat16


PIECES = ((0, 48), (48, 32), (80, 48), (128, 32))
NQ = len(PIECES)


def kernel(
    re_h, rs_h, sh_h, cnt_h, xin_h, g_h, u_h, e_h, prob_h, mst_h, fst_h, snd_h, up_h,
    gi_o, sc_o, nm_o, nf_o, ns_o, nw_o,
    re, rs, cnt, prob, xin, g_in, u_in, e_in, mst, fst, snd, shared,
    w_gate, w_up, dgate, dup, sc_row, sc_tile, sc_recv, comb,
    tmp, keep, r1_send, r1_recv, r2_send, r2_recv, r3_send, r3_recv,
    sg_a, rg_a, sg_b, rg_b, sg, rg, gi_v, sc_v, nm_v, nf_v, ns_v, nw_v,
    in_sem, out_sem, ag_s, ag_r, a2_s, a2_r, sc_s, sc_r, r1_s, r1_r, r2_s, r2_r, r3_s, r3_r,
    ng_s, ng_r,
):
    ep = lax.axis_index("ep")
    dp = lax.axis_index("dp")
    y, x, k = dp // 8, lax.rem(dp // 2, 4), lax.rem(dp, 2)

    def at(yy, xx, kk):
        return yy * 8 + lax.rem(xx + 4, 4) * 2 + kk

    sib, yp, xr, xl, x2 = at(y, x, 1 - k), at(1 - y, x, k), at(y, x + 1, k), at(y, x - 1, k), at(y, x + 2, k)
    yxr, yxl, yx2 = at(1 - y, x + 1, k), at(1 - y, x - 1, k), at(1 - y, x + 2, k)

    def remote(src, dst, s, r, dst_dp):
        return pltpu.make_async_remote_copy(
            src_ref=src, dst_ref=dst, send_sem=s, recv_sem=r,
            device_id=(ep, dst_dp), device_id_type=MESH)

    def rows_of(slot, q=None):
        if q is None:
            return pl.ds(pl.multiple_of(slot * BLK, BLK), BLK)
        return pl.ds(pl.multiple_of(slot * BLK + PIECES[q][0], 16), PIECES[q][1])

    loads = []

    def load(src, dst):
        c = pltpu.make_async_copy(src, dst, in_sem.at[len(loads)])
        c.start()
        loads.append(c)
        return c

    l_mst = load(mst_h.at[0], mst)
    l_up = load(up_h.at[0], w_up.at[rows_of(dp)])
    l_g = load(g_h.at[0], g_in)
    l_u = load(u_h.at[0], u_in)
    l_e = load(e_h.at[0], e_in)
    l_cnt = load(cnt_h, cnt)
    l_prob = load(prob_h, prob)
    l_x = load(xin_h.at[0], xin)
    l_re = load(re_h, re)
    l_rs = load(rs_h, rs)
    l_f = load(fst_h.at[0], fst)
    l_s = load(snd_h.at[0], snd)
    l_sh = load(sh_h, shared)

    bar = pltpu.get_barrier_semaphore()
    for peer in (sib, yp, xr, xl, x2):
        pl.semaphore_signal(bar, inc=1, device_id=(ep, peer), device_id_type=MESH)

    def greet(i, _):
        pl.semaphore_signal(bar, inc=1, device_id=(lax.rem(ep + i, EP), dp), device_id_type=MESH)
        return _

    lax.fori_loop(1, EP, greet, 0)

    l_mst.wait()
    for r in range(0, BLK, 32):
        w_gate[pl.ds(pl.multiple_of(dp * BLK + r, 32), 32), :] = mst[pl.ds(r, 32), :].astype(BF16)
    l_up.wait()
    pl.semaphore_wait(bar, 5 + EP - 1)

    plan = (
        (dp, 0, xr), (dp, 1, xr), (dp, 1, xl), (dp, 0, xl),
        (dp, 0, yp), (dp, 1, yp), (dp, 0, sib), (dp, 1, sib),
        (xl, 0, xr), (xr, 1, xl),
        (xl, 0, sib), (xl, 1, sib), (xr, 0, sib), (xr, 1, sib),
        (yp, 0, xr), (yp, 0, xl), (yp, 1, xr), (yp, 1, xl), (yp, 0, sib), (yp, 1, sib),
        (yxl, 0, xr), (yxr, 1, xl),
        (yxl, 0, sib), (yxl, 1, sib), (yxr, 0, sib), (yxr, 1, sib),
        (x2, 0, sib), (x2, 1, sib), (yx2, 0, sib), (yx2, 1, sib),
    )

    def ag(op):
        slot, piece, to = plan[op]
        ref = (w_gate, w_up)[piece].at[rows_of(slot)]
        return remote(ref, ref, ag_s.at[op], ag_r.at[op], to)

    def ag_go(*ops):
        for op in ops:
            ag(op).start()

    def ag_wait(*ops):
        for op in ops:
            ag(op).wait_recv()

    ag_go(0, 2, 4, 1, 3, 5, 6, 7)

    l_g.wait()
    l_u.wait()
    l_e.wait()
    l_cnt.wait()
    l_prob.wait()
    TILE = 2 * CAP

    def hidden(i, carry):
        rows = pl.ds(pl.multiple_of(i * TILE, TILE), TILE)
        gv = g_in[rows, :].astype(F32)
        uv = u_in[rows, :].astype(F32)
        ev = e_in[rows, :].astype(F32)
        row = lax.broadcasted_iota(jnp.int32, (TILE, ROWS), 0) + i * TILE
        lane = lax.broadcasted_iota(jnp.int32, (TILE, ROWS), 1)
        p = jnp.sum(jnp.where(row == lane, prob[...], 0.0), axis=1, keepdims=True)
        row16 = lax.broadcasted_iota(jnp.int32, (TILE, EP), 0)
        second = (row16 >= CAP).astype(jnp.int32)
        block16 = second + 2 * i
        lane16 = lax.broadcasted_iota(jnp.int32, (TILE, EP), 1)
        limit = jnp.sum(jnp.where(block16 == lane16, cnt[...], 0), axis=1, keepdims=True)
        rank = (row16 - CAP * second)[:, :1]
        live = rank < limit
        sg_ = jax.nn.sigmoid(gv)
        act = gv * sg_
        score = jnp.sum(ev * act * uv, axis=1, keepdims=True)
        pe = p * ev
        d_up = (pe * act).astype(BF16)
        d_gate = (pe * uv * sg_ * (1.0 + gv * (1.0 - sg_))).astype(BF16)
        zero = jnp.zeros_like(d_up)
        dup[rows, :] = jnp.where(live, d_up, zero)
        dgate[rows, :] = jnp.where(live, d_gate, zero)
        score = score.astype(BF16).astype(F32)
        lane128 = lax.broadcasted_iota(jnp.int32, (TILE, 128), 1)
        spread = jnp.where(lane128 == rank, score, 0.0)
        sc_row[pl.ds(2 * i, 1), :] = jnp.sum(spread[:CAP], axis=0, keepdims=True)
        sc_row[pl.ds(2 * i + 1, 1), :] = jnp.sum(spread[CAP:], axis=0, keepdims=True)
        return carry

    lax.fori_loop(0, ROWS // TILE, hidden, 0)
    sc_tile[...] = sc_row[...].astype(BF16)

    def sc_copy(i):
        to = lax.rem(ep + i, EP)
        return pltpu.make_async_remote_copy(
            src_ref=sc_tile, dst_ref=sc_recv.at[ep], send_sem=sc_s, recv_sem=sc_r,
            device_id=(to, dp), device_id_type=MESH)

    sc_recv[ep] = sc_tile[...]

    pair, odd = x // 2, lax.rem(x, 2)
    base = CHUNK * (2 * y + pair)
    groups = (
        (sg_a, rg_a, base + odd * 384, 256),
        (sg_b, rg_b, base + (1 - odd) * 256, 384),
        (sg.at[0], rg.at[0], CHUNK * (2 * y + 1 - pair), CHUNK),
        (sg.at[1], rg.at[1], CHUNK * (2 * (1 - y) + pair), CHUNK),
        (sg.at[2], rg.at[2], CHUNK * (2 * (1 - y) + 1 - pair), CHUNK),
    )

    def a2_copy(i, n):
        to = lax.rem(ep + n, EP)
        src, dst = groups[i][:2]
        return pltpu.make_async_remote_copy(
            src_ref=src.at[to], dst_ref=dst.at[ep], send_sem=a2_s.at[i], recv_sem=a2_r.at[i],
            device_id=(to, dp), device_id_type=MESH)

    def a2_all(i, sem):
        ref = groups[i][1].at[pl.ds(0, EP - 1)]
        return pltpu.make_async_copy(ref, ref, sem.at[i])

    def sc_all(sem):
        ref = sc_recv.at[pl.ds(0, EP - 1)]
        return pltpu.make_async_copy(ref, ref, sem)

    def rows_send(i, first, last, odd_step):
        def send(n, carry):
            a2_copy(i, 2 * n + odd_step).start()
            return carry

        lax.fori_loop(first, last, send, 0)

    def rows_out(i, later=False):
        src, dst, col, width = groups[i]
        rows = pl.ds(pl.multiple_of(col, 128), width)
        dims = (((1,), (1,)), ((), ()))
        out = lax.dot_general(dgate[...], w_gate[rows, :], dims, preferred_element_type=F32)
        out = out + lax.dot_general(dup[...], w_up[rows, :], dims, preferred_element_type=F32)
        src[...] = out.reshape(EP, CAP, width).astype(BF16)

        dst[ep] = src[ep]
        rows_send(i, 1, EP // 2, 0)
        if not later:
            rows_send(i, 0, EP // 2, 1)

    l_x.wait()

    def r1_copy(c):
        blocks = pl.ds(pl.multiple_of(2 * c, 2), 2)
        return remote(r1_send.at[blocks], r1_recv.at[blocks], r1_s.at[c], r1_r.at[c], sib)

    def weight_part(i, carry):
        c = lax.rem(2 * (1 - y) + i, NCH)
        cols = pl.ds(pl.multiple_of(c * CHUNK, CHUNK), CHUNK)
        part = lax.dot_general(
            xin[:, cols], dgate[...], (((0,), (0,)), ((), ())), preferred_element_type=F32)
        tmp[...] = part.reshape(4, BLK, H)
        for j in range(2):
            keep[2 * c + j] = tmp[2 * j + k]
            r1_send[2 * c + j] = tmp[2 * j + 1 - k]
        r1_copy(c).start()
        return carry

    def r1_wait(i, carry):
        c = lax.rem(2 * (1 - y) + i, NCH)
        r1_copy(c).wait_recv()
        return carry

    def piece_of(q):
        return pl.ds(*PIECES[q])

    def r2_copy(q):
        rows = piece_of(q)
        return remote(r2_send.at[:, rows], r2_recv.at[:, rows], r2_s.at[q], r2_r.at[q], yp)

    lax.fori_loop(0, 2, weight_part, 0)
    ag_wait(6, 7)
    rows_out(0, later=True)
    lax.fori_loop(2, NCH, weight_part, 0)
    ag_wait(0, 2)
    ag_go(8, 9, 10, 13)
    ag_wait(4)
    ag_go(14, 18)

    lax.fori_loop(0, 2, r1_wait, 0)
    for q in range(NQ):
        rows = piece_of(q)

        def to_partner(n, carry):
            c = 4 * (1 - y) + n
            r2_send[n, rows] = (keep[c, rows] + r1_recv[c, rows]).astype(BF16)
            return carry

        lax.fori_loop(0, 4, to_partner, 0)
        r2_copy(q).start()

    def send_scores(n, carry):
        sc_copy(n).start()
        return carry

    lax.fori_loop(1, EP, send_scores, 0)

    l_re.wait()
    l_rs.wait()
    rank_of = rs[...]
    expert_of = re[...]
    served = (expert_of < EP) & (rank_of < CAP)
    target = jnp.where(served, expert_of * CAP + rank_of, -1)
    row_j = lax.broadcasted_iota(jnp.int32, (ROWS, TOK), 0)
    hits = jnp.zeros((ROWS, TOK), F32)
    for j in range(TOP):
        hits = hits + jnp.where(target[j:j + 1, :] == row_j, 1.0, 0.0)
    comb[...] = hits.T.astype(BF16)

    ag_wait(1, 3)
    ag_go(11, 12)
    ag_wait(5)
    ag_go(17, 16, 15, 19)
    ag_wait(10, 11, 12, 13)
    rows_out(1, later=True)

    def r3_copy(n, q):
        rows = piece_of(q)
        return remote(r3_send.at[n, rows], r3_recv.at[n, rows], r3_s.at[n, q], r3_r.at[n, q],
                      (xr, xl, x2)[n])

    def over_x(q):
        r2_copy(q).wait_recv()
        rows = piece_of(q)
        for n, dx in enumerate((1, 3, 2)):
            xx = lax.rem(x + dx, 4)
            c = 4 * y + xx
            r3_send[n, rows] = (
                keep[c, rows] + r1_recv[c, rows] + r2_recv[xx, rows].astype(F32)
            ).astype(BF16)
            r3_copy(n, q).start()

    outs = []

    def store(src, dst):
        c = pltpu.make_async_copy(src, dst, out_sem.at[len(outs)])
        c.start()
        outs.append(c)

    ng_plan = (
        (dp, 0, xr), (dp, 0, xl), (dp, 0, yp), (dp, 0, sib),
        (xl, 0, xr), (xl, 0, sib), (xr, 0, sib),
        (yp, 0, xr), (yp, 0, xl), (yp, 0, sib),
        (yxr, 0, xl), (yxl, 0, sib), (yxr, 0, sib), (x2, 0, sib), (yx2, 0, sib),
        (dp, 1, xr), (dp, 1, xl), (dp, 1, yp), (dp, 1, sib),
        (xr, 1, xl), (xr, 1, yp), (xr, 1, sib), (xl, 1, yp), (xl, 1, sib),
        (x2, 1, yp), (x2, 1, sib), (yp, 1, sib), (yxr, 1, sib), (yxl, 1, sib), (yx2, 1, sib),
    )

    def ng(op, pair_of):
        slot, kind, to = ng_plan[op]
        q = 2 * pair_of + kind
        ref = nw_o.at[0, rows_of(slot, q)]
        src = nw_v.at[piece_of(q)] if slot is dp else ref
        return remote(src, ref, ng_s.at[op, pair_of], ng_r.at[op, pair_of], to)

    def ng_go(pair_of, *ops):
        for op in ops:
            ng(op, pair_of).start()

    def ng_hop(pair_of, *moves):
        for arrived, *onward in moves:
            ng(arrived, pair_of).wait_recv()
            ng_go(pair_of, *onward)

    def step(q):
        for n in range(3):
            r3_copy(n, q).wait_recv()
        first, size = PIECES[q]

        def adam(i, carry):
            rows = pl.ds(pl.multiple_of(first + i * 16, 16), 16)
            own = 4 * y + x
            wg = keep[own, rows] + r1_recv[own, rows] + r2_recv[x, rows].astype(F32)
            for n in range(3):
                wg = wg + r3_recv[n, rows].astype(F32)
            m1 = first_decay * fst[rows, :].astype(F32) + (1.0 - first_decay) * wg
            m2 = second_decay * snd[rows, :].astype(F32) + (1.0 - second_decay) * wg * wg
            direction = m1 / first_fix / (jnp.sqrt(m2 / second_fix) + adam_eps)
            now = mst[rows, :]
            new = now - learn_rate * (direction + weight_decay * now)
            nm_v[rows, :] = new
            nf_v[rows, :] = m1.astype(BF16)
            ns_v[rows, :] = m2.astype(BF16)
            nw_v[rows, :] = new.astype(BF16)
            return carry

        lax.fori_loop(0, size // 16, adam, 0)

    def a2_sent(i):
        a2_all(i, a2_s).wait()

    def ag_sent():
        for op in range(len(plan)):
            ag(op).wait_send()

    def sums_sent():
        for c in range(NCH):
            r1_copy(c).wait_send()
        for q in range(NQ):
            r2_copy(q).wait_send()
            for n in range(3):
                r3_copy(n, q).wait_send()
        sc_all(sc_s).wait()

    def tokens(i):
        _, got, col, width = groups[i]

        a2_all(i, a2_r).wait()
        rows = got[...].astype(F32).reshape(ROWS, width).astype(BF16)
        routed = jnp.dot(comb[...], rows, preferred_element_type=F32)
        cols = pl.ds(pl.multiple_of(col, 128), width)
        gi_v[:, cols] = (shared[:, cols].astype(F32) + routed).astype(BF16)
        store(gi_v.at[:, cols], gi_o.at[:, cols])

    def scores_out():
        sc_all(sc_r).wait()
        source = lax.broadcasted_iota(jnp.int32, (EP, EP, 128), 1)
        mine = jnp.sum(jnp.where(source == ep, sc_recv[...].astype(F32), 0.0), axis=1).astype(BF16)
        row_e = lax.broadcasted_iota(jnp.int32, (EP, TOK), 0)
        row_q = lax.broadcasted_iota(jnp.int32, (128, TOK), 0)
        row_k = lax.broadcasted_iota(jnp.int32, (8, TOK), 0)
        result = jnp.zeros((8, TOK), F32)
        for j in range(TOP):
            pick = jnp.where(expert_of[j:j + 1, :] == row_e, 1.0, 0.0).astype(BF16)
            scores = lax.dot_general(mine, pick, (((0,), (0,)), ((), ())), preferred_element_type=F32)
            hit = jnp.where(served[j:j + 1, :], rank_of[j:j + 1, :], -1) == row_q
            value = jnp.sum(jnp.where(hit, scores, 0.0), axis=0, keepdims=True)
            result = jnp.where(row_k == j, value, result)
        sc_v[...] = result[:TOP].astype(BF16)
        store(sc_v, sc_o)

    l_f.wait()
    l_s.wait()
    l_sh.wait()
    lax.fori_loop(2, NCH, r1_wait, 0)

    ag_wait(8, 9)
    ag_go(26, 27)
    ag_wait(26, 27)
    rows_out(2)
    ag_wait(14, 17)
    ag_go(20, 21, 22, 25)
    over_x(0)
    over_x(1)
    ag_wait(15, 16)
    ag_go(24, 23)
    ag_wait(18, 19, 22, 23, 24, 25)
    rows_out(3)
    rows_send(0, 0, EP // 2, 1)
    rows_send(1, 0, EP // 2, 1)
    scores_out()
    ag_wait(20, 21)
    ag_go(28, 29)
    over_x(2)
    over_x(3)
    ag_wait(28, 29)
    rows_out(4)
    step(0)
    ng_go(0, 0, 1, 2, 3)
    step(1)
    ng_go(0, 15, 16, 17, 18)
    step(2)
    ng_go(1, 0, 1, 2, 3)
    ng_hop(0, (0, 4, 5), (2, 7, 8, 9), (16, 19, 20, 21), (15, 22, 23), (1, 6))
    step(3)
    ng_go(1, 15, 16, 17, 18)
    ng_hop(1, (0, 4, 5), (2, 7, 8, 9), (16, 19, 20, 21), (15, 22, 23), (1, 6))
    tokens(0)
    ag_sent()
    ng_hop(0, (8, 10, 12), (19, 24, 25), (7, 11), (4, 13), (17, 26), (20, 27), (22, 28))
    tokens(1)
    a2_sent(0)
    a2_sent(1)
    a2_sent(2)
    ng_hop(1, (8, 10, 12), (19, 24, 25), (7, 11), (4, 13), (17, 26), (20, 27), (22, 28))
    store(nw_v, nw_o.at[0, rows_of(dp)])
    store(nm_v, nm_o.at[0])
    store(nf_v, nf_o.at[0])
    store(ns_v, ns_o.at[0])
    tokens(2)
    ng_hop(0, (10, 14), (24, 29))
    ng_hop(1, (10, 14), (24, 29))
    tokens(3)
    sums_sent()
    a2_sent(3)
    tokens(4)
    for n in range(2):
        ng_hop(n, *((op,) for op in (3, 5, 6, 9, 11, 12, 13, 14, 18, 21, 23, 25, 26, 27, 28, 29)))

    a2_sent(4)
    for op in range(len(ng_plan)):
        for n in range(2):
            ng(op, n).wait_send()
    for c in outs:
        c.wait()


def finish(*refs):
    n = (len(refs) - 2) // 3
    srcs, dsts, held, in_sem, out_sem = refs[:n], refs[n:2 * n], refs[2 * n:3 * n], refs[-2], refs[-1]
    ins, outs = [], []
    for src, dst, mid in zip(srcs, dsts, held):
        rows = src.shape[-2]
        parts = 8 if rows == D else 4 if rows == TOK else 1
        for i in range(parts):
            part = pl.ds(i * (rows // parts), rows // parts)
            index = (0, part) if len(src.shape) == 3 else (part,)
            m = len(ins)
            ins.append(pltpu.make_async_copy(src.at[index], mid.at[index], in_sem.at[m]))
            outs.append(pltpu.make_async_copy(mid.at[index], dst.at[index], out_sem.at[m]))
    for c in ins:
        c.start()
    for c, o in zip(ins, outs):
        c.wait()
        o.start()
    for o in outs:
        o.wait()


def per_device(route_experts, route_slots, *args):
    any_spec = pl.BlockSpec(memory_space=pl.ANY)
    dma = pltpu.SemaphoreType.DMA
    V = pltpu.VMEM
    scratch = [
        V((TOP, TOK), jnp.int32), V((TOP, TOK), jnp.int32), V((1, EP), jnp.int32), V((1, ROWS), F32),
        V((ROWS, D), BF16), V((ROWS, H), BF16), V((ROWS, H), BF16), V((ROWS, H), BF16),
        V((BLK, H), F32), V((BLK, H), BF16), V((BLK, H), BF16), V((TOK, D), BF16),
        V((D, H), BF16), V((D, H), BF16), V((ROWS, H), BF16), V((ROWS, H), BF16),
        V((EP, 128), F32), V((EP, 128), BF16), V((EP, EP, 128), BF16), V((TOK, ROWS), BF16),
        V((4, BLK, H), F32), V((8, BLK, H), F32), V((8, BLK, H), F32), V((8, BLK, H), F32),
        V((4, BLK, H), BF16), V((4, BLK, H), BF16), V((3, BLK, H), BF16), V((3, BLK, H), BF16),
        V((EP, CAP, 256), BF16), V((EP, CAP, 256), BF16), V((EP, CAP, 384), BF16), V((EP, CAP, 384), BF16),
        V((3, EP, CAP, CHUNK), BF16), V((3, EP, CAP, CHUNK), BF16),
        V((TOK, D), BF16), V((TOP, TOK), BF16), V((BLK, H), F32), V((BLK, H), BF16),
        V((BLK, H), BF16), V((BLK, H), BF16),
        dma((13,)), dma((10,)), dma((30,)), dma((30,)), dma((5,)), dma((5,)),
        dma, dma, dma((NCH,)), dma((NCH,)), dma((NQ,)), dma((NQ,)), dma((3, NQ)), dma((3, NQ)),
        dma((30, 2)), dma((30, 2)),
    ]
    shapes = [
        jax.ShapeDtypeStruct((TOK, D), BF16), jax.ShapeDtypeStruct((TOP, TOK), BF16),
        jax.ShapeDtypeStruct((1, BLK, H), F32), jax.ShapeDtypeStruct((1, BLK, H), BF16),
        jax.ShapeDtypeStruct((1, BLK, H), BF16), jax.ShapeDtypeStruct((1, D, H), BF16),
    ]
    parts = pl.pallas_call(
        kernel,
        out_shape=shapes,
        in_specs=[any_spec] * 13,
        out_specs=[any_spec] * 6,
        scratch_shapes=scratch,
        compiler_params=pltpu.CompilerParams(
            collective_id=0, has_side_effects=True, vmem_limit_bytes=60 * 2**20),
        name="backward_tail",
    )(route_experts.T, route_slots.T, *args)
    grad, score, *rest = pl.pallas_call(
        finish,
        out_shape=shapes,
        in_specs=[any_spec] * 6,
        out_specs=[any_spec] * 6,
        scratch_shapes=[V(t.shape, t.dtype) for t in shapes] + [dma((16,)), dma((16,))],
        compiler_params=pltpu.CompilerParams(vmem_limit_bytes=60 * 2**20),
        name="finish",
    )(*parts)
    return (grad, score.T, *rest)


def solution(mesh):
    in_specs = (
        P(("ep", "dp"), None),
        P(("ep", "dp"), None),
        P(("ep", "dp"), None),
        P("ep", "dp"),
        P("ep", "dp", None),
        P("ep", "dp", None),
        P("ep", "dp", None),
        P("ep", "dp", None),
        P("ep", "dp"),
        P("ep", "dp", None),
        P("ep", "dp", None),
        P("ep", "dp", None),
        P("ep", "dp", None),
    )
    out_specs = (
        P(("ep", "dp"), None),
        P(("ep", "dp"), None),
        P("ep", "dp", None),
        P("ep", "dp", None),
        P("ep", "dp", None),
        P("ep", None, None),
    )
    return jax.shard_map(
        per_device, mesh=mesh, in_specs=in_specs, out_specs=out_specs, check_vma=False
    )
```

```python
import jax
import jax.numpy as jnp
from jax import lax
from jax.experimental import pallas as pl
from jax.experimental.pallas import tpu as pltpu
from jax.sharding import PartitionSpec as P

first_decay = 0.9
second_decay = 0.95
learn_rate = 0.001
weight_decay = 0.1
adam_eps = 1e-08
first_fix = 1.0 - 0.9**10
second_fix = 1.0 - 0.95**10

D = 2560
H = 768
CAP = 24
EP = 16
DP = 16
ROWS = EP * CAP
TOK = 256
TOP = 6
BLK = D // DP
CHUNK = 640
NCH = D // CHUNK
MESH = pl.DeviceIdType.MESH
F32 = jnp.float32
BF16 = jnp.bfloat16


PIECES = ((0, 48), (48, 32), (80, 48), (128, 32))
NQ = len(PIECES)


def kernel(
    re_h, rs_h, sh_h, cnt_h, xin_h, g_h, u_h, e_h, prob_h, mst_h, fst_h, snd_h, up_h,
    gi_o, sc_o, nm_o, nf_o, ns_o, nw_o,
    re, rs, cnt, prob, xin, g_in, u_in, e_in, mst, fst, snd, shared,
    w_gate, w_up, dgate, dup, sc_row, sc_tile, sc_recv, comb,
    tmp, keep, r1_send, r1_recv, r2_send, r2_recv, r3_send, r3_recv,
    sg_a, rg_a, sg_b, rg_b, sg, rg, gi_v, sc_v, nm_v, nf_v, ns_v, nw_v,
    in_sem, out_sem, ag_s, ag_r, a2_s, a2_r, sc_s, sc_r, r1_s, r1_r, r2_s, r2_r, r3_s, r3_r,
    ng_s, ng_r,
):
    ep = lax.axis_index("ep")
    dp = lax.axis_index("dp")
    y, x, k = dp // 8, lax.rem(dp // 2, 4), lax.rem(dp, 2)

    def at(yy, xx, kk):
        return yy * 8 + lax.rem(xx + 4, 4) * 2 + kk

    sib, yp, xr, xl, x2 = at(y, x, 1 - k), at(1 - y, x, k), at(y, x + 1, k), at(y, x - 1, k), at(y, x + 2, k)
    yxr, yxl, yx2 = at(1 - y, x + 1, k), at(1 - y, x - 1, k), at(1 - y, x + 2, k)

    def remote(src, dst, s, r, dst_dp):
        return pltpu.make_async_remote_copy(
            src_ref=src, dst_ref=dst, send_sem=s, recv_sem=r,
            device_id=(ep, dst_dp), device_id_type=MESH)

    def rows_of(slot, q=None):
        if q is None:
            return pl.ds(pl.multiple_of(slot * BLK, BLK), BLK)
        return pl.ds(pl.multiple_of(slot * BLK + PIECES[q][0], 16), PIECES[q][1])

    loads = []

    def load(src, dst):
        c = pltpu.make_async_copy(src, dst, in_sem.at[len(loads)])
        c.start()
        loads.append(c)
        return c

    l_mst = load(mst_h.at[0], mst)
    l_up = load(up_h.at[0], w_up.at[rows_of(dp)])
    l_g = load(g_h.at[0], g_in)
    l_u = load(u_h.at[0], u_in)
    l_e = load(e_h.at[0], e_in)
    l_cnt = load(cnt_h, cnt)
    l_prob = load(prob_h, prob)
    l_x = load(xin_h.at[0], xin)
    l_re = load(re_h, re)
    l_rs = load(rs_h, rs)
    l_f = load(fst_h.at[0], fst)
    l_s = load(snd_h.at[0], snd)
    l_sh = load(sh_h, shared)

    bar = pltpu.get_barrier_semaphore()
    for peer in (sib, yp, xr, xl, x2):
        pl.semaphore_signal(bar, inc=1, device_id=(ep, peer), device_id_type=MESH)

    def greet(i, _):
        pl.semaphore_signal(bar, inc=1, device_id=(lax.rem(ep + i, EP), dp), device_id_type=MESH)
        return _

    lax.fori_loop(1, EP, greet, 0)

    l_mst.wait()
    for r in range(0, BLK, 32):
        w_gate[pl.ds(pl.multiple_of(dp * BLK + r, 32), 32), :] = mst[pl.ds(r, 32), :].astype(BF16)
    l_up.wait()
    pl.semaphore_wait(bar, 5 + EP - 1)

    plan = (
        (dp, 0, xr), (dp, 1, xr), (dp, 1, xl), (dp, 0, xl),
        (dp, 0, yp), (dp, 1, yp), (dp, 0, sib), (dp, 1, sib),
        (xl, 0, xr), (xr, 1, xl),
        (xl, 0, sib), (xl, 1, sib), (xr, 0, sib), (xr, 1, sib),
        (yp, 0, xr), (yp, 0, xl), (yp, 1, xr), (yp, 1, xl), (yp, 0, sib), (yp, 1, sib),
        (yxl, 0, xr), (yxr, 1, xl),
        (yxl, 0, sib), (yxl, 1, sib), (yxr, 0, sib), (yxr, 1, sib),
        (x2, 0, sib), (x2, 1, sib), (yx2, 0, sib), (yx2, 1, sib),
    )

    def ag(op):
        slot, piece, to = plan[op]
        ref = (w_gate, w_up)[piece].at[rows_of(slot)]
        return remote(ref, ref, ag_s.at[op], ag_r.at[op], to)

    def ag_go(*ops):
        for op in ops:
            ag(op).start()

    def ag_wait(*ops):
        for op in ops:
            ag(op).wait_recv()

    ag_go(0, 2, 4, 1, 3, 5, 6, 7)

    l_g.wait()
    l_u.wait()
    l_e.wait()
    l_cnt.wait()
    l_prob.wait()
    TILE = 2 * CAP

    def hidden(i, carry):
        rows = pl.ds(pl.multiple_of(i * TILE, TILE), TILE)
        gv = g_in[rows, :].astype(F32)
        uv = u_in[rows, :].astype(F32)
        ev = e_in[rows, :].astype(F32)
        row = lax.broadcasted_iota(jnp.int32, (TILE, ROWS), 0) + i * TILE
        lane = lax.broadcasted_iota(jnp.int32, (TILE, ROWS), 1)
        p = jnp.sum(jnp.where(row == lane, prob[...], 0.0), axis=1, keepdims=True)
        row16 = lax.broadcasted_iota(jnp.int32, (TILE, EP), 0)
        second = (row16 >= CAP).astype(jnp.int32)
        block16 = second + 2 * i
        lane16 = lax.broadcasted_iota(jnp.int32, (TILE, EP), 1)
        limit = jnp.sum(jnp.where(block16 == lane16, cnt[...], 0), axis=1, keepdims=True)
        rank = (row16 - CAP * second)[:, :1]
        live = rank < limit
        sg_ = jax.nn.sigmoid(gv)
        act = gv * sg_
        score = jnp.sum(ev * act * uv, axis=1, keepdims=True)
        pe = p * ev
        d_up = (pe * act).astype(BF16)
        d_gate = (pe * uv * sg_ * (1.0 + gv * (1.0 - sg_))).astype(BF16)
        zero = jnp.zeros_like(d_up)
        dup[rows, :] = jnp.where(live, d_up, zero)
        dgate[rows, :] = jnp.where(live, d_gate, zero)
        score = score.astype(BF16).astype(F32)
        lane128 = lax.broadcasted_iota(jnp.int32, (TILE, 128), 1)
        spread = jnp.where(lane128 == rank, score, 0.0)
        sc_row[pl.ds(2 * i, 1), :] = jnp.sum(spread[:CAP], axis=0, keepdims=True)
        sc_row[pl.ds(2 * i + 1, 1), :] = jnp.sum(spread[CAP:], axis=0, keepdims=True)
        return carry

    lax.fori_loop(0, ROWS // TILE, hidden, 0)
    sc_tile[...] = sc_row[...].astype(BF16)

    def sc_copy(i):
        to = lax.rem(ep + i, EP)
        return pltpu.make_async_remote_copy(
            src_ref=sc_tile, dst_ref=sc_recv.at[ep], send_sem=sc_s, recv_sem=sc_r,
            device_id=(to, dp), device_id_type=MESH)

    sc_recv[ep] = sc_tile[...]

    pair, odd = x // 2, lax.rem(x, 2)
    base = CHUNK * (2 * y + pair)
    groups = (
        (sg_a, rg_a, base + odd * 384, 256),
        (sg_b, rg_b, base + (1 - odd) * 256, 384),
        (sg.at[0], rg.at[0], CHUNK * (2 * y + 1 - pair), CHUNK),
        (sg.at[1], rg.at[1], CHUNK * (2 * (1 - y) + pair), CHUNK),
        (sg.at[2], rg.at[2], CHUNK * (2 * (1 - y) + 1 - pair), CHUNK),
    )

    def a2_copy(i, n):
        to = lax.rem(ep + n, EP)
        src, dst = groups[i][:2]
        return pltpu.make_async_remote_copy(
            src_ref=src.at[to], dst_ref=dst.at[ep], send_sem=a2_s.at[i], recv_sem=a2_r.at[i],
            device_id=(to, dp), device_id_type=MESH)

    def a2_all(i, sem):
        ref = groups[i][1].at[pl.ds(0, EP - 1)]
        return pltpu.make_async_copy(ref, ref, sem.at[i])

    def sc_all(sem):
        ref = sc_recv.at[pl.ds(0, EP - 1)]
        return pltpu.make_async_copy(ref, ref, sem)

    def rows_send(i, first, last, odd_step):
        def send(n, carry):
            a2_copy(i, 2 * n + odd_step).start()
            return carry

        lax.fori_loop(first, last, send, 0)

    def rows_out(i, later=False):
        src, dst, col, width = groups[i]
        rows = pl.ds(pl.multiple_of(col, 128), width)
        dims = (((1,), (1,)), ((), ()))
        out = lax.dot_general(dgate[...], w_gate[rows, :], dims, preferred_element_type=F32)
        out = out + lax.dot_general(dup[...], w_up[rows, :], dims, preferred_element_type=F32)
        src[...] = out.reshape(EP, CAP, width).astype(BF16)

        dst[ep] = src[ep]
        rows_send(i, 1, EP // 2, 0)
        if not later:
            rows_send(i, 0, EP // 2, 1)

    l_x.wait()

    def r1_copy(c):
        blocks = pl.ds(pl.multiple_of(2 * c, 2), 2)
        return remote(r1_send.at[blocks], r1_recv.at[blocks], r1_s.at[c], r1_r.at[c], sib)

    def weight_part(i, carry):
        c = lax.rem(2 * (1 - y) + i, NCH)
        cols = pl.ds(pl.multiple_of(c * CHUNK, CHUNK), CHUNK)
        part = lax.dot_general(
            xin[:, cols], dgate[...], (((0,), (0,)), ((), ())), preferred_element_type=F32)
        tmp[...] = part.reshape(4, BLK, H)
        for j in range(2):
            keep[2 * c + j] = tmp[2 * j + k]
            r1_send[2 * c + j] = tmp[2 * j + 1 - k]
        r1_copy(c).start()
        return carry

    def r1_wait(i, carry):
        c = lax.rem(2 * (1 - y) + i, NCH)
        r1_copy(c).wait_recv()
        return carry

    def piece_of(q):
        return pl.ds(*PIECES[q])

    def r2_copy(q):
        rows = piece_of(q)
        return remote(r2_send.at[:, rows], r2_recv.at[:, rows], r2_s.at[q], r2_r.at[q], yp)

    ag_wait(6, 7)
    rows_out(0, later=True)
    lax.fori_loop(0, 2, weight_part, 0)
    lax.fori_loop(2, NCH, weight_part, 0)
    ag_wait(0, 2)
    ag_go(8, 9, 10, 13)
    ag_wait(4)
    ag_go(14, 18)

    lax.fori_loop(0, 2, r1_wait, 0)
    for q in range(NQ):
        rows = piece_of(q)

        def to_partner(n, carry):
            c = 4 * (1 - y) + n
            r2_send[n, rows] = (keep[c, rows] + r1_recv[c, rows]).astype(BF16)
            return carry

        lax.fori_loop(0, 4, to_partner, 0)
        r2_copy(q).start()

    def send_scores(n, carry):
        sc_copy(n).start()
        return carry

    lax.fori_loop(1, EP, send_scores, 0)

    l_re.wait()
    l_rs.wait()
    rank_of = rs[...]
    expert_of = re[...]
    served = (expert_of < EP) & (rank_of < CAP)
    target = jnp.where(served, expert_of * CAP + rank_of, -1)
    row_j = lax.broadcasted_iota(jnp.int32, (ROWS, TOK), 0)
    hits = jnp.zeros((ROWS, TOK), F32)
    for j in range(TOP):
        hits = hits + jnp.where(target[j:j + 1, :] == row_j, 1.0, 0.0)
    comb[...] = hits.T.astype(BF16)

    ag_wait(1, 3)
    ag_go(11, 12)
    ag_wait(5)
    ag_go(17, 16, 15, 19)
    ag_wait(10, 11, 12, 13)
    rows_out(1, later=True)

    def r3_copy(n, q):
        rows = piece_of(q)
        return remote(r3_send.at[n, rows], r3_recv.at[n, rows], r3_s.at[n, q], r3_r.at[n, q],
                      (xr, xl, x2)[n])

    def over_x(q):
        r2_copy(q).wait_recv()
        rows = piece_of(q)
        for n, dx in enumerate((1, 3, 2)):
            xx = lax.rem(x + dx, 4)
            c = 4 * y + xx
            r3_send[n, rows] = (
                keep[c, rows] + r1_recv[c, rows] + r2_recv[xx, rows].astype(F32)
            ).astype(BF16)
            r3_copy(n, q).start()

    outs = []

    def store(src, dst):
        c = pltpu.make_async_copy(src, dst, out_sem.at[len(outs)])
        c.start()
        outs.append(c)

    ng_plan = (
        (dp, 0, xr), (dp, 0, xl), (dp, 0, yp), (dp, 0, sib),
        (xl, 0, xr), (xl, 0, sib), (xr, 0, sib),
        (yp, 0, xr), (yp, 0, xl), (yp, 0, sib),
        (yxr, 0, xl), (yxl, 0, sib), (yxr, 0, sib), (x2, 0, sib), (yx2, 0, sib),
        (dp, 1, xr), (dp, 1, xl), (dp, 1, yp), (dp, 1, sib),
        (xr, 1, xl), (xr, 1, yp), (xr, 1, sib), (xl, 1, yp), (xl, 1, sib),
        (x2, 1, yp), (x2, 1, sib), (yp, 1, sib), (yxr, 1, sib), (yxl, 1, sib), (yx2, 1, sib),
    )

    def ng(op, pair_of):
        slot, kind, to = ng_plan[op]
        q = 2 * pair_of + kind
        ref = nw_o.at[0, rows_of(slot, q)]
        src = nw_v.at[piece_of(q)] if slot is dp else ref
        return remote(src, ref, ng_s.at[op, pair_of], ng_r.at[op, pair_of], to)

    def ng_go(pair_of, *ops):
        for op in ops:
            ng(op, pair_of).start()

    def ng_hop(pair_of, *moves):
        for arrived, *onward in moves:
            ng(arrived, pair_of).wait_recv()
            ng_go(pair_of, *onward)

    def step(q):
        for n in range(3):
            r3_copy(n, q).wait_recv()
        first, size = PIECES[q]

        def adam(i, carry):
            rows = pl.ds(pl.multiple_of(first + i * 16, 16), 16)
            own = 4 * y + x
            wg = keep[own, rows] + r1_recv[own, rows] + r2_recv[x, rows].astype(F32)
            for n in range(3):
                wg = wg + r3_recv[n, rows].astype(F32)
            m1 = first_decay * fst[rows, :].astype(F32) + (1.0 - first_decay) * wg
            m2 = second_decay * snd[rows, :].astype(F32) + (1.0 - second_decay) * wg * wg
            direction = m1 / first_fix / (jnp.sqrt(m2 / second_fix) + adam_eps)
            now = mst[rows, :]
            new = now - learn_rate * (direction + weight_decay * now)
            nm_v[rows, :] = new
            nf_v[rows, :] = m1.astype(BF16)
            ns_v[rows, :] = m2.astype(BF16)
            nw_v[rows, :] = new.astype(BF16)
            return carry

        lax.fori_loop(0, size // 16, adam, 0)

    def a2_sent(i):
        a2_all(i, a2_s).wait()

    def ag_sent():
        for op in range(len(plan)):
            ag(op).wait_send()

    def sums_sent():
        for c in range(NCH):
            r1_copy(c).wait_send()
        for q in range(NQ):
            r2_copy(q).wait_send()
            for n in range(3):
                r3_copy(n, q).wait_send()
        sc_all(sc_s).wait()

    def tokens(i):
        _, got, col, width = groups[i]

        a2_all(i, a2_r).wait()
        rows = got[...].astype(F32).reshape(ROWS, width).astype(BF16)
        routed = jnp.dot(comb[...], rows, preferred_element_type=F32)
        cols = pl.ds(pl.multiple_of(col, 128), width)
        gi_v[:, cols] = (shared[:, cols].astype(F32) + routed).astype(BF16)
        store(gi_v.at[:, cols], gi_o.at[:, cols])

    def scores_out():
        sc_all(sc_r).wait()
        source = lax.broadcasted_iota(jnp.int32, (EP, EP, 128), 1)
        mine = jnp.sum(jnp.where(source == ep, sc_recv[...].astype(F32), 0.0), axis=1).astype(BF16)
        row_e = lax.broadcasted_iota(jnp.int32, (EP, TOK), 0)
        row_q = lax.broadcasted_iota(jnp.int32, (128, TOK), 0)
        row_k = lax.broadcasted_iota(jnp.int32, (8, TOK), 0)
        result = jnp.zeros((8, TOK), F32)
        for j in range(TOP):
            pick = jnp.where(expert_of[j:j + 1, :] == row_e, 1.0, 0.0).astype(BF16)
            scores = lax.dot_general(mine, pick, (((0,), (0,)), ((), ())), preferred_element_type=F32)
            hit = jnp.where(served[j:j + 1, :], rank_of[j:j + 1, :], -1) == row_q
            value = jnp.sum(jnp.where(hit, scores, 0.0), axis=0, keepdims=True)
            result = jnp.where(row_k == j, value, result)
        sc_v[...] = result[:TOP].astype(BF16)
        store(sc_v, sc_o)

    l_f.wait()
    l_s.wait()
    l_sh.wait()
    lax.fori_loop(2, NCH, r1_wait, 0)

    ag_wait(8, 9)
    ag_go(26, 27)
    ag_wait(26, 27)
    rows_out(2)
    ag_wait(14, 17)
    ag_go(20, 21, 22, 25)
    over_x(0)
    over_x(1)
    ag_wait(15, 16)
    ag_go(24, 23)
    ag_wait(18, 19, 22, 23, 24, 25)
    rows_out(3)
    rows_send(0, 0, EP // 2, 1)
    rows_send(1, 0, EP // 2, 1)
    scores_out()
    ag_wait(20, 21)
    ag_go(28, 29)
    over_x(2)
    over_x(3)
    ag_wait(28, 29)
    rows_out(4)
    step(0)
    ng_go(0, 0, 1, 2, 3)
    step(1)
    ng_go(0, 15, 16, 17, 18)
    step(2)
    ng_go(1, 0, 1, 2, 3)
    ng_hop(0, (0, 4, 5), (2, 7, 8, 9), (16, 19, 20, 21), (15, 22, 23), (1, 6))
    step(3)
    ng_go(1, 15, 16, 17, 18)
    ng_hop(1, (0, 4, 5), (2, 7, 8, 9), (16, 19, 20, 21), (15, 22, 23), (1, 6))
    tokens(0)
    ag_sent()
    ng_hop(0, (8, 10, 12), (19, 24, 25), (7, 11), (4, 13), (17, 26), (20, 27), (22, 28))
    tokens(1)
    a2_sent(0)
    a2_sent(1)
    a2_sent(2)
    ng_hop(1, (8, 10, 12), (19, 24, 25), (7, 11), (4, 13), (17, 26), (20, 27), (22, 28))
    store(nw_v, nw_o.at[0, rows_of(dp)])
    store(nm_v, nm_o.at[0])
    store(nf_v, nf_o.at[0])
    store(ns_v, ns_o.at[0])
    tokens(2)
    ng_hop(0, (10, 14), (24, 29))
    ng_hop(1, (10, 14), (24, 29))
    tokens(3)
    sums_sent()
    a2_sent(3)
    tokens(4)
    for n in range(2):
        ng_hop(n, *((op,) for op in (3, 5, 6, 9, 11, 12, 13, 14, 18, 21, 23, 25, 26, 27, 28, 29)))

    a2_sent(4)
    for op in range(len(ng_plan)):
        for n in range(2):
            ng(op, n).wait_send()
    for c in outs:
        c.wait()


def finish(*refs):
    n = (len(refs) - 2) // 3
    srcs, dsts, held, in_sem, out_sem = refs[:n], refs[n:2 * n], refs[2 * n:3 * n], refs[-2], refs[-1]
    ins, outs = [], []
    for src, dst, mid in zip(srcs, dsts, held):
        rows = src.shape[-2]
        parts = 8 if rows == D else 4 if rows == TOK else 1
        for i in range(parts):
            part = pl.ds(i * (rows // parts), rows // parts)
            index = (0, part) if len(src.shape) == 3 else (part,)
            m = len(ins)
            ins.append(pltpu.make_async_copy(src.at[index], mid.at[index], in_sem.at[m]))
            outs.append(pltpu.make_async_copy(mid.at[index], dst.at[index], out_sem.at[m]))
    for c in ins:
        c.start()
    for c, o in zip(ins, outs):
        c.wait()
        o.start()
    for o in outs:
        o.wait()


def per_device(route_experts, route_slots, *args):
    any_spec = pl.BlockSpec(memory_space=pl.ANY)
    dma = pltpu.SemaphoreType.DMA
    V = pltpu.VMEM
    scratch = [
        V((TOP, TOK), jnp.int32), V((TOP, TOK), jnp.int32), V((1, EP), jnp.int32), V((1, ROWS), F32),
        V((ROWS, D), BF16), V((ROWS, H), BF16), V((ROWS, H), BF16), V((ROWS, H), BF16),
        V((BLK, H), F32), V((BLK, H), BF16), V((BLK, H), BF16), V((TOK, D), BF16),
        V((D, H), BF16), V((D, H), BF16), V((ROWS, H), BF16), V((ROWS, H), BF16),
        V((EP, 128), F32), V((EP, 128), BF16), V((EP, EP, 128), BF16), V((TOK, ROWS), BF16),
        V((4, BLK, H), F32), V((8, BLK, H), F32), V((8, BLK, H), F32), V((8, BLK, H), F32),
        V((4, BLK, H), BF16), V((4, BLK, H), BF16), V((3, BLK, H), BF16), V((3, BLK, H), BF16),
        V((EP, CAP, 256), BF16), V((EP, CAP, 256), BF16), V((EP, CAP, 384), BF16), V((EP, CAP, 384), BF16),
        V((3, EP, CAP, CHUNK), BF16), V((3, EP, CAP, CHUNK), BF16),
        V((TOK, D), BF16), V((TOP, TOK), BF16), V((BLK, H), F32), V((BLK, H), BF16),
        V((BLK, H), BF16), V((BLK, H), BF16),
        dma((13,)), dma((10,)), dma((30,)), dma((30,)), dma((5,)), dma((5,)),
        dma, dma, dma((NCH,)), dma((NCH,)), dma((NQ,)), dma((NQ,)), dma((3, NQ)), dma((3, NQ)),
        dma((30, 2)), dma((30, 2)),
    ]
    shapes = [
        jax.ShapeDtypeStruct((TOK, D), BF16), jax.ShapeDtypeStruct((TOP, TOK), BF16),
        jax.ShapeDtypeStruct((1, BLK, H), F32), jax.ShapeDtypeStruct((1, BLK, H), BF16),
        jax.ShapeDtypeStruct((1, BLK, H), BF16), jax.ShapeDtypeStruct((1, D, H), BF16),
    ]
    parts = pl.pallas_call(
        kernel,
        out_shape=shapes,
        in_specs=[any_spec] * 13,
        out_specs=[any_spec] * 6,
        scratch_shapes=scratch,
        compiler_params=pltpu.CompilerParams(
            collective_id=0, has_side_effects=True, vmem_limit_bytes=60 * 2**20),
        name="backward_tail",
    )(route_experts.T, route_slots.T, *args)
    grad, score, *rest = pl.pallas_call(
        finish,
        out_shape=shapes,
        in_specs=[any_spec] * 6,
        out_specs=[any_spec] * 6,
        scratch_shapes=[V(t.shape, t.dtype) for t in shapes] + [dma((16,)), dma((16,))],
        compiler_params=pltpu.CompilerParams(vmem_limit_bytes=60 * 2**20),
        name="finish",
    )(*parts)
    return (grad, score.T, *rest)


def solution(mesh):
    in_specs = (
        P(("ep", "dp"), None),
        P(("ep", "dp"), None),
        P(("ep", "dp"), None),
        P("ep", "dp"),
        P("ep", "dp", None),
        P("ep", "dp", None),
        P("ep", "dp", None),
        P("ep", "dp", None),
        P("ep", "dp"),
        P("ep", "dp", None),
        P("ep", "dp", None),
        P("ep", "dp", None),
        P("ep", "dp", None),
    )
    out_specs = (
        P(("ep", "dp"), None),
        P(("ep", "dp"), None),
        P("ep", "dp", None),
        P("ep", "dp", None),
        P("ep", "dp", None),
        P("ep", None, None),
    )
    return jax.shard_map(
        per_device, mesh=mesh, in_specs=in_specs, out_specs=out_specs, check_vma=False
    )
```
